256 devices in a mesh: pipe: 4 (over x), seq: 64 (over z, y, core).
Axes of the slice: x: 4, y: 4, z: 8, core: 2. Of those that a mesh axis runs over, the one named last changes fastest.
Arguments:
- query_latent: bfloat16 [4, 1024, 64, 512], P('pipe', 'seq'), may hold values from -32 to 32
- query_rope: bfloat16 [4, 1024, 4096], P('pipe', 'seq'), may hold values from -4 to 4
- key_latent: bfloat16 [4, 1024, 512], P('pipe', 'seq'), may hold values from -8 to 8
- key_rope: bfloat16 [4, 1024, 64], P('pipe', 'seq'), may hold values from -4 to 4
- positions: int32 [4, 1024], P('pipe', 'seq'), may hold values from -1 to 8191, as said below
- router_weight: float32 [4, 1024], P('pipe', 'seq'), may hold values from 0.2 to 1
- value_up: bfloat16 [4, 64, 512, 128], P('pipe'), may hold values from -1.5 to 1.5
Outputs:
- handed: bfloat16 [4, 1024, 8192], P('pipe', 'seq')
The draws below stay inside these ranges and needn't reach their ends.
Inputs may be any that keep to these rules, and one draw needn't show every extreme that they name: Within a section, each device's block of 16 slots (the device with seq index i holds positions in [i * 128, (i + 1) * 128)) has its live rows first, positions strictly rising, then empty slots holding -1. At least 8 slots of every block are live, and in every section some block has all 16 slots live.
All inputs are finite; a program needn't handle non-finite values.
Results may differ from the reference program's by a relative error of at most 0.007.
Values may be sent and summed in bfloat16 or wider, within the bound.
A program may use at most 64 MiB of HBM per device.

```python
import jax
import jax.numpy as jnp
from jax import lax

HEADS = 64
LAT = 512
ROPE = 64
VD = 128
ROWS = 16
SECTIONS = 4
NR = 1024
TOK_DEV = 128
N_SEQ = 64


def latent_draw(key):
    values_draw = jnp.clip(jax.random.normal(jax.random.fold_in(key, 11), (SECTIONS, NR, LAT), jnp.float32), -4.0, 4.0)
    return values_draw


def draw_key_latent(key, part):
    return latent_draw(key).astype(jnp.bfloat16)


def draw_query_latent(key, part):
    values_draw = jnp.clip(jax.random.normal(jax.random.fold_in(key, 22), (SECTIONS, NR, HEADS, LAT), jnp.float32), -4.0, 4.0)
    return values_draw.astype(jnp.bfloat16)


def draw_positions(key, part):
    count_key = jax.random.fold_in(key, 31)
    full_key = jax.random.fold_in(key, 32)
    rank_key = jax.random.fold_in(key, 33)
    counts = jax.random.randint(count_key, (SECTIONS, N_SEQ), ROWS // 2, ROWS + 1)
    full_dev = jax.random.randint(full_key, (SECTIONS, 1), 0, N_SEQ)
    counts = jnp.where(jnp.arange(N_SEQ)[None, :] == full_dev, ROWS, counts)
    ranking = jax.random.randint(rank_key, (SECTIONS, N_SEQ, TOK_DEV), 0, 1048576) * TOK_DEV + jnp.arange(TOK_DEV)[None, None, :]
    chosen = jnp.argsort(ranking, axis=-1, stable=True)[:, :, :ROWS].astype(jnp.int32)
    chosen = jnp.sort(chosen, axis=-1)
    slot_index = jnp.arange(ROWS)[None, None, :]
    live_slot = slot_index < counts[:, :, None]
    offset_base = jnp.arange(N_SEQ, dtype=jnp.int32)[None, :, None] * TOK_DEV
    placed = jnp.where(live_slot, chosen + offset_base, -1)
    return placed.reshape(SECTIONS, NR).astype(jnp.int32)


def shard_levels(own_key, shape, cuts, smallest, high):
    def one(position, shards_of):
        heights = jax.random.uniform(jax.random.fold_in(jax.random.fold_in(own_key, 6), position), (shards_of,), jnp.float32, smallest / len(cuts), high / len(cuts))
        return jnp.repeat(jnp.exp(heights), shape[position] // shards_of).reshape((-1,) + (1,) * (len(shape) - position - 1))

    level = one(*cuts[0])
    for cut in cuts[1:]:
        level = level * one(*cut)
    return level


def bell_draw(own_key, extent, deviation, reach, shards=(), kind=jnp.bfloat16):
    entries = deviation * jax.random.normal(own_key, extent, jnp.float32)
    if shards:
        entries = entries * shard_levels(own_key, extent, shards, -0.22, 0.18)
    return jnp.clip(entries, -reach, reach).astype(kind)


def setup_inputs(seed: int = 0) -> dict:
    arg_keys = jax.random.split(jax.random.key(seed), 8)
    query_latent = draw_query_latent(jax.random.fold_in(arg_keys[7], 71), 0)
    query_rope = bell_draw(arg_keys[1], (SECTIONS, NR, HEADS * ROPE), 1.0, 4.0, ((0, 4), (1, 64)))
    key_latent = draw_key_latent(jax.random.fold_in(arg_keys[7], 71), 0)
    key_rope = bell_draw(arg_keys[3], (SECTIONS, NR, ROPE), 1.0, 4.0, ((0, 4), (1, 64)))
    positions = draw_positions(jax.random.fold_in(arg_keys[7], 71), 0)
    router_weight = jnp.clip(0.2 + 0.8 * jax.random.uniform(arg_keys[5], (SECTIONS, NR), jnp.float32) ** shard_levels(arg_keys[5], (SECTIONS, NR), ((0, 4), (1, 64)), -0.2, 0.2), 0.2, 1.0)
    value_up = bell_draw(arg_keys[6], (SECTIONS, HEADS, LAT, VD), (max(LAT // 32, 1)) ** -0.5, 1.5, ((0, 4),))
    return dict(query_latent=query_latent, query_rope=query_rope, key_latent=key_latent, key_rope=key_rope, positions=positions, router_weight=router_weight, value_up=value_up)


SOFTMAX_SCALE = 0.07216878364870322
MASKED = -1.0e30


def section_result(query_latent, query_rope, key_latent, key_rope, positions, router_weight, value_up):
    total_rows = query_latent.shape[0]
    head_count = query_latent.shape[1]
    rope_query = query_rope.reshape(total_rows, head_count, -1)
    block_len = min(total_rows, 512)
    value_map = value_up.astype(jnp.float32)
    pieces = []
    for start_row in range(0, total_rows, block_len):
        finish = start_row + block_len
        query_block = query_latent[start_row:finish].astype(jnp.float32)
        rope_block = rope_query[start_row:finish].astype(jnp.float32)
        key_block = key_latent[:finish].astype(jnp.float32)
        key_rope_block = key_rope[:finish].astype(jnp.float32)
        scores = jnp.einsum("qhl,kl->qhk", query_block, key_block) + jnp.einsum("qhr,kr->qhk", rope_block, key_rope_block)
        scores = scores * SOFTMAX_SCALE
        query_pos = positions[start_row:finish]
        key_pos = positions[:finish]
        visible = (key_pos[None, :] >= 0) & (key_pos[None, :] <= query_pos[:, None])
        scores = jnp.where(visible[:, None, :], scores, MASKED)
        largest = jnp.max(scores, axis=2, keepdims=True)
        exp_terms = jnp.where(visible[:, None, :], jnp.exp(scores - largest), 0.0)
        denominator = jnp.sum(exp_terms, axis=2)
        weights = lax.optimization_barrier(exp_terms.astype(jnp.bfloat16)).astype(jnp.float32)
        summed = jnp.einsum("qhk,kl->qhl", weights, key_block)
        latent = summed / jnp.maximum(denominator, 1.0)[:, :, None]
        latent = lax.optimization_barrier(latent.astype(jnp.bfloat16)).astype(jnp.float32)
        projected = jnp.einsum("qhl,hlv->qhv", latent, value_map)
        gated = projected.reshape(finish - start_row, -1) * router_weight[start_row:finish][:, None]
        pieces.append(gated.astype(jnp.bfloat16))
    return jnp.concatenate(pieces, axis=0)


def reference(query_latent, query_rope, key_latent, key_rope, positions, router_weight, value_up):
    section_outs = []
    for section_index in range(SECTIONS):
        section_outs.append(section_result(query_latent[section_index], query_rope[section_index], key_latent[section_index], key_rope[section_index], positions[section_index], router_weight[section_index], value_up[section_index]))
    stacked = jnp.stack(section_outs, axis=0)
    return jnp.roll(stacked, 1, axis=0)
```

```python
import jax
import jax.numpy as jnp
from jax import lax
from jax.experimental import pallas as pl
from jax.experimental.pallas import tpu as pltpu
from jax.sharding import PartitionSpec as P

SCALE_LOG2E = 0.07216878364870322 * 1.4426950408889634
MASKED = -1.0e30
ROWS = 16
HEADS = 64
LAT = 512
ROPE = 64
VD = 128
NZ = 8
NY = 4
WIDE = LAT + 128
ZROW = NY * 2 * ROWS
KEYS = NZ * ZROW
GROUP = 16
GROUP_ROWS = GROUP * ROWS
N_GROUPS = HEADS // GROUP
PIECE = 4
MESH = pl.DeviceIdType.MESH
PLACE = {0: 0, 7: 1, 1: 2, 6: 3, 2: 4, 5: 5, 3: 6, 4: 7}
NEAR_FIRST = (7, 1, 6, 2, 5, 3, 4)


def body(
    ql_hbm, qr_hbm, kl_hbm, kr_hbm, pos_hbm, rw_hbm, vu_hbm, out_hbm,
    ql, qr, kl, kr, pos, rw, vu, q, kv, res,
    local_sem, vu_sem, a_send, a_recv, y_send, y_recv, c_send, c_recv, x_send, x_recv,
):
    seq = lax.axis_index("seq")
    pipe = lax.axis_index("pipe")
    z = seq // (NY * 2)
    y = (seq // 2) % NY
    c = seq % 2

    def at(zz, yy, cc):
        return {"seq": (zz * NY + yy) * 2 + cc}

    def y_peer(dy):
        return at(z, (y + dy) % NY, c)

    sibling = at(z, y, 1 - c)
    after = {"pipe": (pipe + 1) % 4}
    before = {"pipe": (pipe + 3) % 4}

    barrier = pltpu.get_barrier_semaphore()
    for t in range(1, NZ):

        @pl.when(z - t >= 0)
        def _():
            pl.semaphore_signal(barrier, inc=1, device_id=at(z - t, y, c), device_id_type=MESH)

    for dy in (1, 2, 3):
        pl.semaphore_signal(barrier, inc=1, device_id=y_peer(dy), device_id_type=MESH)
    pl.semaphore_signal(barrier, inc=1, device_id=sibling, device_id_type=MESH)
    pl.semaphore_signal(barrier, inc=1, device_id=before, device_id_type=MESH)

    loads = [
        pltpu.make_async_copy(kl_hbm.at[0], kl, local_sem.at[0]),
        pltpu.make_async_copy(kr_hbm.at[0], kr, local_sem.at[1]),
        pltpu.make_async_copy(pos_hbm, pos, local_sem.at[2]),
        pltpu.make_async_copy(rw_hbm, rw, local_sem.at[3]),
        pltpu.make_async_copy(ql_hbm.at[0], ql, local_sem.at[4]),
        pltpu.make_async_copy(qr_hbm.at[0], qr, local_sem.at[5]),
    ]
    for load in loads:
        load.start()

    def vu_load(g):
        return pltpu.make_async_copy(
            vu_hbm.at[0, pl.ds(g * GROUP, GROUP)], vu.at[pl.ds(g * GROUP, GROUP)], vu_sem.at[g]
        )

    diagonal = lax.broadcasted_iota(jnp.int32, (ROWS, ROWS), 0) == lax.broadcasted_iota(
        jnp.int32, (ROWS, ROWS), 1
    )
    for load in loads[:4]:
        load.wait()
    live_lane = jnp.where(pos[...] >= 0, 1.0, 0.0)
    live = jnp.sum(jnp.where(diagonal, live_lane, 0.0), axis=1, keepdims=True)
    gate = jnp.sum(jnp.where(diagonal, rw[...], 0.0), axis=1, keepdims=True) * live
    lane = lax.broadcasted_iota(jnp.int32, (ROWS, 128), 1)
    bias = jnp.where(live > 0.5, 0.0, MASKED)
    place = c * (NY * ROWS) + y * ROWS
    own_rows = pl.ds(pl.multiple_of(place, ROWS), ROWS)
    kv[own_rows, :LAT] = kl[...]
    kv[own_rows, LAT:] = jnp.where(
        lane < ROPE,
        jnp.concatenate([kr[...].astype(jnp.float32), jnp.zeros((ROWS, 128 - ROPE), jnp.float32)], axis=1),
        jnp.where(lane == ROPE, bias, 0.0),
    ).astype(jnp.bfloat16)

    pl.semaphore_wait(barrier, (NZ - 1 - z) + 5)

    def rows_of(dz):
        return pl.ds(pl.multiple_of(PLACE[dz] * ZROW + place, ROWS), ROWS)

    def half_of(dz, cc):
        return pl.ds(pl.multiple_of(PLACE[dz] * ZROW + cc * (NY * ROWS), ROWS), NY * ROWS)

    def a_copy(t):
        return pltpu.make_async_remote_copy(
            src_ref=kv.at[own_rows],
            dst_ref=kv.at[rows_of(NZ - t)],
            send_sem=a_send.at[t - 1],
            recv_sem=a_recv.at[NZ - t - 1],
            device_id=at(z + t, y, c),
            device_id_type=MESH,
        )

    def a_arrival(dz):
        return pltpu.make_async_remote_copy(
            src_ref=kv.at[own_rows],
            dst_ref=kv.at[rows_of(dz)],
            send_sem=a_send.at[0],
            recv_sem=a_recv.at[dz - 1],
            device_id=sibling,
            device_id_type=MESH,
        )

    def y_copy(dz, dy):
        return pltpu.make_async_remote_copy(
            src_ref=kv.at[rows_of(dz)],
            dst_ref=kv.at[rows_of(dz)],
            send_sem=y_send.at[dz, dy - 1],
            recv_sem=y_recv.at[dz, dy - 1],
            device_id=y_peer(dy),
            device_id_type=MESH,
        )

    def c_copy(dz):
        return pltpu.make_async_remote_copy(
            src_ref=kv.at[half_of(dz, c)],
            dst_ref=kv.at[half_of(dz, c)],
            send_sem=c_send.at[dz],
            recv_sem=c_recv.at[dz],
            device_id=sibling,
            device_id_type=MESH,
        )

    for t in (1, 2, 3, 4, 5, 6, 7):

        @pl.when(z + t < NZ)
        def _():
            a_copy(t).start()

    for dy in (1, 3, 2):
        y_copy(0, dy).start()
    for g in range(N_GROUPS):
        vu_load(g).start()

    tail_tile = jnp.where(lax.broadcasted_iota(jnp.int32, (ZROW, 128), 1) == ROPE, MASKED, 0.0).astype(jnp.bfloat16)
    for dz in NEAR_FIRST:

        @pl.when(z + dz < NZ)
        def _():
            rows = pl.ds(PLACE[dz] * ZROW, ZROW)
            kv[rows, :LAT] = jnp.zeros((ZROW, LAT), jnp.bfloat16)
            kv[rows, LAT:] = tail_tile

    for load in loads[4:]:
        load.wait()
    out_row = lax.broadcasted_iota(jnp.int32, (GROUP_ROWS, GROUP_ROWS), 0)
    in_row = lax.broadcasted_iota(jnp.int32, (GROUP_ROWS, GROUP_ROWS), 1)
    shuffle = ((out_row % ROWS) * GROUP + out_row // ROWS == in_row).astype(jnp.bfloat16)
    for g in range(N_GROUPS):
        block = ql[:, g * GROUP : (g + 1) * GROUP, :].reshape(GROUP_ROWS, LAT)
        q[g * GROUP_ROWS : (g + 1) * GROUP_ROWS, :LAT] = jnp.dot(
            shuffle, block, preferred_element_type=jnp.float32
        ).astype(jnp.bfloat16)
    for j in range(HEADS // 2):
        pair = qr[:, j * 128 : (j + 1) * 128].astype(jnp.float32)
        for odd in (0, 1):
            part = pltpu.roll(pair, ROPE, 1) if odd else pair
            part = jnp.where(lane < ROPE, part, jnp.where(lane == ROPE, 1.0, 0.0))
            h = 2 * j + odd
            q[h * ROWS : (h + 1) * ROWS, LAT:] = part.astype(jnp.bfloat16)

    def on_a(dz):
        @pl.when(z + dz >= NZ)
        def _():
            a_arrival(dz).wait_recv()
            for dy in (1, 3, 2):
                y_copy(dz, dy).start()

    def on_y(dz):
        def go():
            for dy in (1, 3, 2):
                y_copy(dz, dy).wait_recv()
            c_copy(dz).start()

        if dz == 0:
            go()
        else:
            pl.when(z + dz >= NZ)(go)

    on_a(7)
    on_a(1)
    on_y(0)
    on_a(6)
    on_a(2)
    on_a(5)
    on_a(3)
    on_y(7)
    on_y(1)
    on_a(4)
    on_y(6)
    on_y(2)
    on_y(5)
    on_y(3)
    on_y(4)
    c_copy(0).wait_recv()
    for dz in NEAR_FIRST:

        @pl.when(z + dz >= NZ)
        def _():
            c_copy(dz).wait_recv()

    key_slot = lax.broadcasted_iota(jnp.int32, (GROUP_ROWS, ZROW), 1)
    key_index = ((key_slot // ROWS) % NY) * (2 * ROWS) + (key_slot // (NY * ROWS)) * ROWS + key_slot % ROWS
    query_index = (y * 2 + c) * ROWS + lax.broadcasted_iota(jnp.int32, (GROUP_ROWS, ZROW), 0) % ROWS
    seen = key_index <= query_index

    def x_copy(p):
        columns = pl.ds(pl.multiple_of(p * (PIECE * VD), 128), PIECE * VD)
        return pltpu.make_async_remote_copy(
            src_ref=res.at[:, columns],
            dst_ref=out_hbm.at[0, :, columns],
            send_sem=x_send.at[p],
            recv_sem=x_recv.at[p],
            device_id=after,
            device_id_type=MESH,
        )

    @pl.loop(0, N_GROUPS)
    def _(g):
        rows = pl.ds(pl.multiple_of(g * GROUP_ROWS, GROUP_ROWS), GROUP_ROWS)
        scores = lax.dot_general(
            q[rows, :], kv[...], (((1,), (1,)), ((), ())), preferred_element_type=jnp.float32
        )
        scores = jnp.concatenate([jnp.where(seen, scores[:, :ZROW], MASKED), scores[:, ZROW:]], axis=1)
        top = jnp.max(scores, axis=1, keepdims=True)
        terms = jnp.exp2((scores - top) * SCALE_LOG2E)
        total = jnp.sum(terms, axis=1, keepdims=True)
        summed = jnp.dot(terms.astype(jnp.bfloat16), kv[:, :LAT], preferred_element_type=jnp.float32)
        latent = (summed * (1.0 / jnp.maximum(total, 1.0))).astype(jnp.bfloat16)
        vu_load(g).wait()
        for j in range(GROUP // 2):
            maps = vu[pl.ds(g * GROUP + 2 * j, 2)]
            both = jnp.concatenate([maps[0], maps[1]], axis=1)
            wide = jnp.dot(
                latent[2 * j * ROWS : (2 * j + 2) * ROWS], both, preferred_element_type=jnp.float32
            )
            piece = jnp.concatenate([wide[:ROWS, :VD], wide[ROWS:, VD:]], axis=1) * gate
            columns = pl.ds(pl.multiple_of((g * GROUP + 2 * j) * VD, 128), 2 * VD)
            res[:, columns] = piece.astype(jnp.bfloat16)
            if j % 2 == 1:
                x_copy(g * (GROUP // PIECE) + j // 2).start()

    @pl.loop(0, HEADS // PIECE)
    def _(p):
        x_copy(p).wait()

    for t in (1, 2, 3, 4, 5, 6, 7):

        @pl.when(z + t < NZ)
        def _():
            a_copy(t).wait_send()

    for dz in (0,) + NEAR_FIRST:

        def done():
            for dy in (1, 3, 2):
                y_copy(dz, dy).wait_send()
            c_copy(dz).wait_send()

        if dz == 0:
            done()
        else:
            pl.when(z + dz >= NZ)(done)


def on_device(query_latent, query_rope, key_latent, key_rope, positions, router_weight, value_up):
    return pl.pallas_call(
        body,
        out_shape=jax.ShapeDtypeStruct((1, ROWS, HEADS * VD), jnp.bfloat16),
        in_specs=[pl.BlockSpec(memory_space=pltpu.HBM)] * 7,
        out_specs=pl.BlockSpec(memory_space=pltpu.HBM),
        scratch_shapes=[
            pltpu.VMEM((ROWS, HEADS, LAT), jnp.bfloat16),
            pltpu.VMEM((ROWS, HEADS * ROPE), jnp.bfloat16),
            pltpu.VMEM((ROWS, LAT), jnp.bfloat16),
            pltpu.VMEM((ROWS, ROPE), jnp.bfloat16),
            pltpu.VMEM((1, ROWS), jnp.int32),
            pltpu.VMEM((1, ROWS), jnp.float32),
            pltpu.VMEM((HEADS, LAT, VD), jnp.bfloat16),
            pltpu.VMEM((HEADS * ROWS, WIDE), jnp.bfloat16),
            pltpu.VMEM((KEYS, WIDE), jnp.bfloat16),
            pltpu.VMEM((ROWS, HEADS * VD), jnp.bfloat16),
            pltpu.SemaphoreType.DMA((6,)),
            pltpu.SemaphoreType.DMA((N_GROUPS,)),
            pltpu.SemaphoreType.DMA((NZ - 1,)),
            pltpu.SemaphoreType.DMA((NZ - 1,)),
            pltpu.SemaphoreType.DMA((NZ, 3)),
            pltpu.SemaphoreType.DMA((NZ, 3)),
            pltpu.SemaphoreType.DMA((NZ,)),
            pltpu.SemaphoreType.DMA((NZ,)),
            pltpu.SemaphoreType.DMA((HEADS // PIECE,)),
            pltpu.SemaphoreType.DMA((HEADS // PIECE,)),
        ],
        compiler_params=pltpu.CompilerParams(
            collective_id=0, has_side_effects=True, vmem_limit_bytes=48 * 2**20
        ),
        cost_estimate=pl.CostEstimate(flops=2_400_000_000, bytes_accessed=11_000_000, transcendentals=1_048_576),
        name="attend_and_hand_on",
    )(query_latent, query_rope, key_latent, key_rope, positions, router_weight, value_up)


def solution(mesh):
    placed = (
        P("pipe", "seq", None, None),
        P("pipe", "seq", None),
        P("pipe", "seq", None),
        P("pipe", "seq", None),
        P("pipe", "seq"),
        P("pipe", "seq"),
        P("pipe", None, None, None),
    )
    return jax.shard_map(
        on_device, mesh=mesh, in_specs=placed, out_specs=P("pipe", "seq", None), check_vma=False
    )
```

```python
import jax
import jax.numpy as jnp
from jax import lax
from jax.experimental import pallas as pl
from jax.experimental.pallas import tpu as pltpu
from jax.sharding import PartitionSpec as P

SCALE_LOG2E = 0.07216878364870322 * 1.4426950408889634
MASKED = -1.0e30
ROWS = 16
HEADS = 64
LAT = 512
ROPE = 64
VD = 128
NZ = 8
NY = 4
WIDE = LAT + 128
ZROW = NY * 2 * ROWS
KEYS = NZ * ZROW
GROUP = 16
GROUP_ROWS = GROUP * ROWS
N_GROUPS = HEADS // GROUP
PIECE = 4
MESH = pl.DeviceIdType.MESH
PLACE = {0: 0, 7: 1, 1: 2, 6: 3, 2: 4, 5: 5, 3: 6, 4: 7}
NEAR_FIRST = (7, 1, 6, 2, 5, 3, 4)
FAR = (4, 3, 5, 2, 6)
EARLY = 4 * ZROW


def body(
    ql_hbm, qr_hbm, kl_hbm, kr_hbm, pos_hbm, rw_hbm, vu_hbm, out,
    ql, qr, kl, kr, pos, rw, vu, q, kv, res, early,
    local_sem, vu_sem, a_send, a_recv, y_send, y_recv, c_send, c_recv, x_send, x_recv,
):
    seq = lax.axis_index("seq")
    pipe = lax.axis_index("pipe")
    z = seq // (NY * 2)
    y = (seq // 2) % NY
    c = seq % 2

    def at(zz, yy, cc):
        return {"seq": (zz * NY + yy) * 2 + cc}

    def y_peer(dy):
        return at(z, (y + dy) % NY, c)

    sibling = at(z, y, 1 - c)
    after = {"pipe": (pipe + 1) % 4}
    before = {"pipe": (pipe + 3) % 4}

    barrier = pltpu.get_barrier_semaphore()
    for t in range(1, NZ):

        @pl.when(z - t >= 0)
        def _():
            pl.semaphore_signal(barrier, inc=1, device_id=at(z - t, y, c), device_id_type=MESH)

    for dy in (1, 2, 3):
        pl.semaphore_signal(barrier, inc=1, device_id=y_peer(dy), device_id_type=MESH)
    pl.semaphore_signal(barrier, inc=1, device_id=sibling, device_id_type=MESH)
    pl.semaphore_signal(barrier, inc=1, device_id=before, device_id_type=MESH)

    loads = [
        pltpu.make_async_copy(kl_hbm.at[0], kl, local_sem.at[0]),
        pltpu.make_async_copy(kr_hbm.at[0], kr, local_sem.at[1]),
        pltpu.make_async_copy(pos_hbm, pos, local_sem.at[2]),
        pltpu.make_async_copy(rw_hbm, rw, local_sem.at[3]),
        pltpu.make_async_copy(ql_hbm.at[0], ql, local_sem.at[4]),
        pltpu.make_async_copy(qr_hbm.at[0], qr, local_sem.at[5]),
    ]
    for load in loads:
        load.start()

    def vu_load(g):
        return pltpu.make_async_copy(
            vu_hbm.at[0, pl.ds(g * GROUP, GROUP)], vu.at[pl.ds(g * GROUP, GROUP)], vu_sem.at[g]
        )

    diagonal = lax.broadcasted_iota(jnp.int32, (ROWS, ROWS), 0) == lax.broadcasted_iota(
        jnp.int32, (ROWS, ROWS), 1
    )
    for load in loads[:4]:
        load.wait()
    live_lane = jnp.where(pos[...] >= 0, 1.0, 0.0)
    live = jnp.sum(jnp.where(diagonal, live_lane, 0.0), axis=1, keepdims=True)
    gate = jnp.sum(jnp.where(diagonal, rw[...], 0.0), axis=1, keepdims=True) * live
    lane = lax.broadcasted_iota(jnp.int32, (ROWS, 128), 1)
    bias = jnp.where(live > 0.5, 0.0, MASKED)
    place = c * (NY * ROWS) + y * ROWS
    own_rows = pl.ds(pl.multiple_of(place, ROWS), ROWS)
    kv[own_rows, :LAT] = kl[...]
    kv[own_rows, LAT:] = jnp.where(
        lane < ROPE,
        jnp.concatenate([kr[...].astype(jnp.float32), jnp.zeros((ROWS, 128 - ROPE), jnp.float32)], axis=1),
        jnp.where(lane == ROPE, bias, 0.0),
    ).astype(jnp.bfloat16)

    pl.semaphore_wait(barrier, (NZ - 1 - z) + 5)

    def rows_of(dz):
        return pl.ds(pl.multiple_of(PLACE[dz] * ZROW + place, ROWS), ROWS)

    def half_of(dz, cc):
        return pl.ds(pl.multiple_of(PLACE[dz] * ZROW + cc * (NY * ROWS), ROWS), NY * ROWS)

    def a_copy(t):
        return pltpu.make_async_remote_copy(
            src_ref=kv.at[own_rows],
            dst_ref=kv.at[rows_of(NZ - t)],
            send_sem=a_send.at[t - 1],
            recv_sem=a_recv.at[NZ - t - 1],
            device_id=at(z + t, y, c),
            device_id_type=MESH,
        )

    def d_copy(t):
        return pltpu.make_async_remote_copy(
            src_ref=kv.at[half_of(0, c)],
            dst_ref=kv.at[half_of(NZ - t, c)],
            send_sem=a_send.at[t - 1],
            recv_sem=a_recv.at[NZ - t - 1],
            device_id=at(z + t, y, c),
            device_id_type=MESH,
        )

    def d_arrival(dz):
        return pltpu.make_async_remote_copy(
            src_ref=kv.at[half_of(0, c)],
            dst_ref=kv.at[half_of(dz, c)],
            send_sem=a_send.at[0],
            recv_sem=a_recv.at[dz - 1],
            device_id=sibling,
            device_id_type=MESH,
        )

    def a_arrival(dz):
        return pltpu.make_async_remote_copy(
            src_ref=kv.at[own_rows],
            dst_ref=kv.at[rows_of(dz)],
            send_sem=a_send.at[0],
            recv_sem=a_recv.at[dz - 1],
            device_id=sibling,
            device_id_type=MESH,
        )

    def y_copy(dz, dy):
        return pltpu.make_async_remote_copy(
            src_ref=kv.at[rows_of(dz)],
            dst_ref=kv.at[rows_of(dz)],
            send_sem=y_send.at[dz, dy - 1],
            recv_sem=y_recv.at[dz, dy - 1],
            device_id=y_peer(dy),
            device_id_type=MESH,
        )

    def c_copy(dz):
        return pltpu.make_async_remote_copy(
            src_ref=kv.at[half_of(dz, c)],
            dst_ref=kv.at[half_of(dz, c)],
            send_sem=c_send.at[dz],
            recv_sem=c_recv.at[dz],
            device_id=sibling,
            device_id_type=MESH,
        )

    for t in FAR:

        @pl.when(z + t < NZ)
        def _():
            a_copy(t).start()

    for dy in (1, 3, 2):
        y_copy(0, dy).start()
    for g in range(N_GROUPS):
        vu_load(g).start()

    tail_tile = jnp.where(lax.broadcasted_iota(jnp.int32, (ZROW, 128), 1) == ROPE, MASKED, 0.0).astype(jnp.bfloat16)
    for dz in NEAR_FIRST:

        @pl.when(z + dz < NZ)
        def _():
            rows = pl.ds(PLACE[dz] * ZROW, ZROW)
            kv[rows, :LAT] = jnp.zeros((ZROW, LAT), jnp.bfloat16)
            kv[rows, LAT:] = tail_tile

    for load in loads[4:]:
        load.wait()
    out_row = lax.broadcasted_iota(jnp.int32, (GROUP_ROWS, GROUP_ROWS), 0)
    in_row = lax.broadcasted_iota(jnp.int32, (GROUP_ROWS, GROUP_ROWS), 1)
    shuffle = ((out_row % ROWS) * GROUP + out_row // ROWS == in_row).astype(jnp.bfloat16)
    for g in range(N_GROUPS):
        block = ql[:, g * GROUP : (g + 1) * GROUP, :].reshape(GROUP_ROWS, LAT)
        q[g * GROUP_ROWS : (g + 1) * GROUP_ROWS, :LAT] = jnp.dot(
            shuffle, block, preferred_element_type=jnp.float32
        ).astype(jnp.bfloat16)
    for j in range(HEADS // 2):
        pair = qr[:, j * 128 : (j + 1) * 128].astype(jnp.float32)
        for odd in (0, 1):
            part = pltpu.roll(pair, ROPE, 1) if odd else pair
            part = jnp.where(lane < ROPE, part, jnp.where(lane == ROPE, 1.0, 0.0))
            h = 2 * j + odd
            q[h * ROWS : (h + 1) * ROWS, LAT:] = part.astype(jnp.bfloat16)

    def on_a(dz):
        @pl.when(z + dz >= NZ)
        def _():
            a_arrival(dz).wait_recv()
            for dy in (1, 3, 2):
                y_copy(dz, dy).start()

    def on_y(dz):
        @pl.when(z + dz >= NZ)
        def _():
            for dy in (1, 3, 2):
                y_copy(dz, dy).wait_recv()
            c_copy(dz).start()

    def on_d(dz):
        @pl.when(z + dz >= NZ)
        def _():
            d_arrival(dz).wait_recv()
            c_copy(dz).start()

    def on_c(dz):
        @pl.when(z + dz >= NZ)
        def _():
            c_copy(dz).wait_recv()

    for dy in (1, 3, 2):
        y_copy(0, dy).wait_recv()
    for t in (1, 7):

        @pl.when(z + t < NZ)
        def _():
            d_copy(t).start()

    c_copy(0).start()
    for dz in (6, 2, 5, 3, 4):
        on_a(dz)
    on_d(7)
    on_d(1)
    for dz in (6, 2, 5, 3, 4):
        on_y(dz)
    c_copy(0).wait_recv()
    for dz in (7, 1, 6):
        on_c(dz)
    early[...] = lax.dot_general(
        q[...], kv[:EARLY], (((1,), (1,)), ((), ())), preferred_element_type=jnp.float32
    )
    for dz in (2, 5, 3, 4):
        on_c(dz)

    key_slot = lax.broadcasted_iota(jnp.int32, (GROUP_ROWS, ZROW), 1)
    key_index = ((key_slot // ROWS) % NY) * (2 * ROWS) + (key_slot // (NY * ROWS)) * ROWS + key_slot % ROWS
    query_index = (y * 2 + c) * ROWS + lax.broadcasted_iota(jnp.int32, (GROUP_ROWS, ZROW), 0) % ROWS
    seen = key_index <= query_index

    def x_copy(p):
        columns = pl.ds(pl.multiple_of(p * (PIECE * VD), 128), PIECE * VD)
        return pltpu.make_async_remote_copy(
            src_ref=res.at[:, columns],
            dst_ref=out.at[0, :, columns],
            send_sem=x_send.at[p],
            recv_sem=x_recv.at[p],
            device_id=after,
            device_id_type=MESH,
        )

    for g in range(N_GROUPS):
        vu_load(g).wait()

    @pl.loop(0, N_GROUPS)
    def _(g):
        rows = pl.ds(pl.multiple_of(g * GROUP_ROWS, GROUP_ROWS), GROUP_ROWS)
        late = lax.dot_general(
            q[rows, :], kv[EARLY:], (((1,), (1,)), ((), ())), preferred_element_type=jnp.float32
        )
        scores = jnp.concatenate(
            [jnp.where(seen, early[rows, :ZROW], MASKED), early[rows, ZROW:], late], axis=1
        )
        top = jnp.max(scores, axis=1, keepdims=True)
        terms = jnp.exp2((scores - top) * SCALE_LOG2E)
        total = jnp.sum(terms, axis=1, keepdims=True)
        summed = jnp.dot(terms.astype(jnp.bfloat16), kv[:, :LAT], preferred_element_type=jnp.float32)
        latent = (summed * (1.0 / jnp.maximum(total, 1.0))).astype(jnp.bfloat16)
        for j in range(GROUP // 2):
            maps = vu[pl.ds(g * GROUP + 2 * j, 2)]
            both = jnp.concatenate([maps[0], maps[1]], axis=1)
            wide = jnp.dot(
                latent[2 * j * ROWS : (2 * j + 2) * ROWS], both, preferred_element_type=jnp.float32
            )
            piece = jnp.concatenate([wide[:ROWS, :VD], wide[ROWS:, VD:]], axis=1) * gate
            columns = pl.ds(pl.multiple_of((g * GROUP + 2 * j) * VD, 128), 2 * VD)
            res[:, columns] = piece.astype(jnp.bfloat16)
            if j % 2 == 1:
                x_copy(g * (GROUP // PIECE) + j // 2).start()

    @pl.loop(0, HEADS // PIECE)
    def _(p):
        x_copy(p).wait()

    for t in FAR:

        @pl.when(z + t < NZ)
        def _():
            a_copy(t).wait_send()

    for t in (1, 7):

        @pl.when(z + t < NZ)
        def _():
            d_copy(t).wait_send()

    for dy in (1, 3, 2):
        y_copy(0, dy).wait_send()
    c_copy(0).wait_send()
    for dz in NEAR_FIRST:

        @pl.when(z + dz >= NZ)
        def _():
            if dz in FAR:
                for dy in (1, 3, 2):
                    y_copy(dz, dy).wait_send()
            c_copy(dz).wait_send()


def on_device(query_latent, query_rope, key_latent, key_rope, positions, router_weight, value_up):
    return pl.pallas_call(
        body,
        out_shape=pltpu.VMEM((1, ROWS, HEADS * VD), jnp.bfloat16),
        in_specs=[pl.BlockSpec(memory_space=pltpu.HBM)] * 7,
        out_specs=pl.BlockSpec(memory_space=pltpu.VMEM),
        scratch_shapes=[
            pltpu.VMEM((ROWS, HEADS, LAT), jnp.bfloat16),
            pltpu.VMEM((ROWS, HEADS * ROPE), jnp.bfloat16),
            pltpu.VMEM((ROWS, LAT), jnp.bfloat16),
            pltpu.VMEM((ROWS, ROPE), jnp.bfloat16),
            pltpu.VMEM((1, ROWS), jnp.int32),
            pltpu.VMEM((1, ROWS), jnp.float32),
            pltpu.VMEM((HEADS, LAT, VD), jnp.bfloat16),
            pltpu.VMEM((HEADS * ROWS, WIDE), jnp.bfloat16),
            pltpu.VMEM((KEYS, WIDE), jnp.bfloat16),
            pltpu.VMEM((ROWS, HEADS * VD), jnp.bfloat16),
            pltpu.VMEM((HEADS * ROWS, EARLY), jnp.float32),
            pltpu.SemaphoreType.DMA((6,)),
            pltpu.SemaphoreType.DMA((N_GROUPS,)),
            pltpu.SemaphoreType.DMA((NZ - 1,)),
            pltpu.SemaphoreType.DMA((NZ - 1,)),
            pltpu.SemaphoreType.DMA((NZ, 3)),
            pltpu.SemaphoreType.DMA((NZ, 3)),
            pltpu.SemaphoreType.DMA((NZ,)),
            pltpu.SemaphoreType.DMA((NZ,)),
            pltpu.SemaphoreType.DMA((HEADS // PIECE,)),
            pltpu.SemaphoreType.DMA((HEADS // PIECE,)),
        ],
        compiler_params=pltpu.CompilerParams(
            collective_id=0, has_side_effects=True, vmem_limit_bytes=56 * 2**20
        ),
        cost_estimate=pl.CostEstimate(flops=2_400_000_000, bytes_accessed=11_000_000, transcendentals=1_048_576),
        name="attend_and_hand_on",
    )(query_latent, query_rope, key_latent, key_rope, positions, router_weight, value_up)


def solution(mesh):
    placed = (
        P("pipe", "seq", None, None),
        P("pipe", "seq", None),
        P("pipe", "seq", None),
        P("pipe", "seq", None),
        P("pipe", "seq"),
        P("pipe", "seq"),
        P("pipe", None, None, None),
    )
    return jax.shard_map(
        on_device, mesh=mesh, in_specs=placed, out_specs=P("pipe", "seq", None), check_vma=False
    )
```

```python
import jax
import jax.numpy as jnp
from jax import lax
from jax.experimental import pallas as pl
from jax.experimental.pallas import tpu as pltpu
from jax.sharding import PartitionSpec as P

SCALE_LOG2E = 0.07216878364870322 * 1.4426950408889634
MASKED = -1.0e30
ROWS = 16
HEADS = 64
LAT = 512
ROPE = 64
VD = 128
NZ = 8
NY = 4
WIDE = LAT + 128
ZROW = NY * 2 * ROWS
KEYS = NZ * ZROW
GROUP = 16
GROUP_ROWS = GROUP * ROWS
N_GROUPS = HEADS // GROUP
PIECE = 16
MESH = pl.DeviceIdType.MESH
PLACE = {0: 0, 7: 1, 1: 2, 6: 3, 2: 4, 5: 5, 3: 6, 4: 7}
NEAR_FIRST = (7, 1, 6, 2, 5, 3, 4)
FAR = (2, 6, 3, 5, 4)
EARLY = 4 * ZROW


def body(
    ql_hbm, qr_hbm, kl_hbm, kr_hbm, pos_hbm, rw_hbm, vu_hbm, out,
    ql, qr, kl, kr, pos, rw, vu, q, kv, res, early, latents,
    local_sem, vu_sem, a_send, a_recv, y_send, y_recv, c_send, c_recv, x_send, x_recv,
):
    seq = lax.axis_index("seq")
    pipe = lax.axis_index("pipe")
    z = seq // (NY * 2)
    y = (seq // 2) % NY
    c = seq % 2

    def at(zz, yy, cc):
        return {"seq": (zz * NY + yy) * 2 + cc}

    def y_peer(dy):
        return at(z, (y + dy) % NY, c)

    sibling = at(z, y, 1 - c)
    after = {"pipe": (pipe + 1) % 4}
    before = {"pipe": (pipe + 3) % 4}

    barrier = pltpu.get_barrier_semaphore()
    for t in (7, 6, 5, 4, 3, 2, 1):

        @pl.when(z - t >= 0)
        def _():
            pl.semaphore_signal(barrier, inc=1, device_id=at(z - t, y, c), device_id_type=MESH)

    for dy in (1, 2, 3):
        pl.semaphore_signal(barrier, inc=1, device_id=y_peer(dy), device_id_type=MESH)
    pl.semaphore_signal(barrier, inc=1, device_id=sibling, device_id_type=MESH)
    pl.semaphore_signal(barrier, inc=1, device_id=before, device_id_type=MESH)

    loads = [
        pltpu.make_async_copy(kl_hbm.at[0], kl, local_sem.at[0]),
        pltpu.make_async_copy(kr_hbm.at[0], kr, local_sem.at[1]),
        pltpu.make_async_copy(pos_hbm, pos, local_sem.at[2]),
        pltpu.make_async_copy(rw_hbm, rw, local_sem.at[3]),
        pltpu.make_async_copy(ql_hbm.at[0], ql, local_sem.at[4]),
        pltpu.make_async_copy(qr_hbm.at[0], qr, local_sem.at[5]),
    ]
    for load in loads:
        load.start()

    def vu_load(g):
        return pltpu.make_async_copy(
            vu_hbm.at[0, pl.ds(g * GROUP, GROUP)], vu.at[pl.ds(g * GROUP, GROUP)], vu_sem.at[g]
        )

    diagonal = lax.broadcasted_iota(jnp.int32, (ROWS, ROWS), 0) == lax.broadcasted_iota(
        jnp.int32, (ROWS, ROWS), 1
    )
    for load in loads[:4]:
        load.wait()
    live_lane = jnp.where(pos[...] >= 0, 1.0, 0.0)
    live = jnp.sum(jnp.where(diagonal, live_lane, 0.0), axis=1, keepdims=True)
    gate = jnp.sum(jnp.where(diagonal, rw[...], 0.0), axis=1, keepdims=True) * live
    lane = lax.broadcasted_iota(jnp.int32, (ROWS, 128), 1)
    bias = jnp.where(live > 0.5, 0.0, MASKED)
    place = c * (NY * ROWS) + y * ROWS
    own_rows = pl.ds(pl.multiple_of(place, ROWS), ROWS)
    kv[own_rows, :LAT] = kl[...]
    kv[own_rows, LAT:] = jnp.where(
        lane < ROPE,
        jnp.concatenate([kr[...].astype(jnp.float32), jnp.zeros((ROWS, 128 - ROPE), jnp.float32)], axis=1),
        jnp.where(lane == ROPE, bias, 0.0),
    ).astype(jnp.bfloat16)

    tail_tile = jnp.where(lax.broadcasted_iota(jnp.int32, (ZROW, 128), 1) == ROPE, MASKED, 0.0).astype(jnp.bfloat16)
    for dz in NEAR_FIRST:

        @pl.when(z + dz < NZ)
        def _():
            rows = pl.ds(PLACE[dz] * ZROW, ZROW)
            kv[rows, :LAT] = jnp.zeros((ZROW, LAT), jnp.bfloat16)
            kv[rows, LAT:] = tail_tile

    for load in loads[4:]:
        load.wait()
    out_row = lax.broadcasted_iota(jnp.int32, (GROUP_ROWS, GROUP_ROWS), 0)
    in_row = lax.broadcasted_iota(jnp.int32, (GROUP_ROWS, GROUP_ROWS), 1)
    shuffle = ((out_row % ROWS) * GROUP + out_row // ROWS == in_row).astype(jnp.bfloat16)
    for g in range(N_GROUPS):
        block = ql[:, g * GROUP : (g + 1) * GROUP, :].reshape(GROUP_ROWS, LAT)
        q[g * GROUP_ROWS : (g + 1) * GROUP_ROWS, :LAT] = jnp.dot(
            shuffle, block, preferred_element_type=jnp.float32
        ).astype(jnp.bfloat16)
    for j in range(HEADS // 2):
        pair = qr[:, j * 128 : (j + 1) * 128].astype(jnp.float32)
        for odd in (0, 1):
            part = pltpu.roll(pair, ROPE, 1) if odd else pair
            part = jnp.where(lane < ROPE, part, jnp.where(lane == ROPE, 1.0, 0.0))
            h = 2 * j + odd
            q[h * ROWS : (h + 1) * ROWS, LAT:] = part.astype(jnp.bfloat16)

    pl.semaphore_wait(barrier, (NZ - 1 - z) + 5)

    def rows_of(dz):
        return pl.ds(pl.multiple_of(PLACE[dz] * ZROW + place, ROWS), ROWS)

    def half_of(dz, cc):
        return pl.ds(pl.multiple_of(PLACE[dz] * ZROW + cc * (NY * ROWS), ROWS), NY * ROWS)

    def a_copy(t):
        return pltpu.make_async_remote_copy(
            src_ref=kv.at[own_rows],
            dst_ref=kv.at[rows_of(NZ - t)],
            send_sem=a_send.at[t - 1],
            recv_sem=a_recv.at[NZ - t - 1],
            device_id=at(z + t, y, c),
            device_id_type=MESH,
        )

    def d_copy(t):
        return pltpu.make_async_remote_copy(
            src_ref=kv.at[half_of(0, c)],
            dst_ref=kv.at[half_of(NZ - t, c)],
            send_sem=a_send.at[t - 1],
            recv_sem=a_recv.at[NZ - t - 1],
            device_id=at(z + t, y, c),
            device_id_type=MESH,
        )

    def d_arrival(dz):
        return pltpu.make_async_remote_copy(
            src_ref=kv.at[half_of(0, c)],
            dst_ref=kv.at[half_of(dz, c)],
            send_sem=a_send.at[0],
            recv_sem=a_recv.at[dz - 1],
            device_id=sibling,
            device_id_type=MESH,
        )

    def a_arrival(dz):
        return pltpu.make_async_remote_copy(
            src_ref=kv.at[own_rows],
            dst_ref=kv.at[rows_of(dz)],
            send_sem=a_send.at[0],
            recv_sem=a_recv.at[dz - 1],
            device_id=sibling,
            device_id_type=MESH,
        )

    def y_copy(dz, dy):
        return pltpu.make_async_remote_copy(
            src_ref=kv.at[rows_of(dz)],
            dst_ref=kv.at[rows_of(dz)],
            send_sem=y_send.at[dz, dy - 1],
            recv_sem=y_recv.at[dz, dy - 1],
            device_id=y_peer(dy),
            device_id_type=MESH,
        )

    def c_copy(dz):
        return pltpu.make_async_remote_copy(
            src_ref=kv.at[half_of(dz, c)],
            dst_ref=kv.at[half_of(dz, c)],
            send_sem=c_send.at[dz],
            recv_sem=c_recv.at[dz],
            device_id=sibling,
            device_id_type=MESH,
        )

    for t in FAR:

        @pl.when(z + t < NZ)
        def _():
            a_copy(t).start()

    for dy in (1, 3, 2):
        y_copy(0, dy).start()
    for g in range(N_GROUPS):
        vu_load(g).start()

    def on_a(dz):
        @pl.when(z + dz >= NZ)
        def _():
            a_arrival(dz).wait_recv()
            for dy in (1, 3, 2):
                y_copy(dz, dy).start()

    def on_y(dz):
        @pl.when(z + dz >= NZ)
        def _():
            for dy in (1, 3, 2):
                y_copy(dz, dy).wait_recv()
            c_copy(dz).start()

    def on_d(dz):
        @pl.when(z + dz >= NZ)
        def _():
            d_arrival(dz).wait_recv()
            c_copy(dz).start()

    def on_c(dz):
        @pl.when(z + dz >= NZ)
        def _():
            c_copy(dz).wait_recv()

    for dy in (1, 3, 2):
        y_copy(0, dy).wait_recv()
    for t in (1, 7):

        @pl.when(z + t < NZ)
        def _():
            d_copy(t).start()

    c_copy(0).start()
    for dz in (6, 2, 5, 3, 4):
        on_a(dz)
    on_d(7)
    on_d(1)
    for dz in (6, 2, 5, 3, 4):
        on_y(dz)
    c_copy(0).wait_recv()
    for dz in (7, 1, 6):
        on_c(dz)
    early[...] = lax.dot_general(
        q[...], kv[:EARLY], (((1,), (1,)), ((), ())), preferred_element_type=jnp.float32
    )
    for dz in (2, 5, 3, 4):
        on_c(dz)

    key_slot = lax.broadcasted_iota(jnp.int32, (GROUP_ROWS, ZROW), 1)
    key_index = ((key_slot // ROWS) % NY) * (2 * ROWS) + (key_slot // (NY * ROWS)) * ROWS + key_slot % ROWS
    query_index = (y * 2 + c) * ROWS + lax.broadcasted_iota(jnp.int32, (GROUP_ROWS, ZROW), 0) % ROWS
    seen = key_index <= query_index

    def x_copy(p):
        columns = pl.ds(pl.multiple_of(p * (PIECE * VD), 128), PIECE * VD)
        return pltpu.make_async_remote_copy(
            src_ref=res.at[:, columns],
            dst_ref=out.at[0, :, columns],
            send_sem=x_send.at[p],
            recv_sem=x_recv.at[p],
            device_id=after,
            device_id_type=MESH,
        )

    for g in range(N_GROUPS):
        vu_load(g).wait()

    @pl.loop(0, N_GROUPS)
    def _(g):
        rows = pl.ds(pl.multiple_of(g * GROUP_ROWS, GROUP_ROWS), GROUP_ROWS)

        def attend(scores, keys):
            top = jnp.max(scores, axis=1, keepdims=True)
            terms = jnp.exp2((scores - top) * SCALE_LOG2E)
            total = jnp.sum(terms, axis=1, keepdims=True)
            summed = jnp.dot(terms.astype(jnp.bfloat16), kv[:keys, :LAT], preferred_element_type=jnp.float32)
            latents[...] = (summed * (1.0 / jnp.maximum(total, 1.0))).astype(jnp.bfloat16)

        def first():
            return jnp.concatenate([jnp.where(seen, early[rows, :ZROW], MASKED), early[rows, ZROW:]], axis=1)

        @pl.when(z >= 3)
        def _():
            late = lax.dot_general(
                q[rows, :], kv[EARLY:], (((1,), (1,)), ((), ())), preferred_element_type=jnp.float32
            )
            attend(jnp.concatenate([first(), late], axis=1), KEYS)

        @pl.when(z < 3)
        def _():
            attend(first(), EARLY)

        latent = latents[...]
        for j in range(GROUP // 2):
            maps = vu[pl.ds(g * GROUP + 2 * j, 2)]
            both = jnp.concatenate([maps[0], maps[1]], axis=1)
            wide = jnp.dot(
                latent[2 * j * ROWS : (2 * j + 2) * ROWS], both, preferred_element_type=jnp.float32
            )
            piece = jnp.concatenate([wide[:ROWS, :VD], wide[ROWS:, VD:]], axis=1) * gate
            columns = pl.ds(pl.multiple_of((g * GROUP + 2 * j) * VD, 128), 2 * VD)
            res[:, columns] = piece.astype(jnp.bfloat16)
            if (2 * j + 2) % PIECE == 0:
                x_copy(g * (GROUP // PIECE) + (2 * j) // PIECE).start()

    @pl.loop(0, HEADS // PIECE)
    def _(p):
        x_copy(p).wait()

    for t in FAR:

        @pl.when(z + t < NZ)
        def _():
            a_copy(t).wait_send()

    for t in (1, 7):

        @pl.when(z + t < NZ)
        def _():
            d_copy(t).wait_send()

    for dy in (1, 3, 2):
        y_copy(0, dy).wait_send()
    c_copy(0).wait_send()
    for dz in NEAR_FIRST:

        @pl.when(z + dz >= NZ)
        def _():
            if dz in FAR:
                for dy in (1, 3, 2):
                    y_copy(dz, dy).wait_send()
            c_copy(dz).wait_send()


def on_device(query_latent, query_rope, key_latent, key_rope, positions, router_weight, value_up):
    return pl.pallas_call(
        body,
        out_shape=pltpu.VMEM((1, ROWS, HEADS * VD), jnp.bfloat16),
        in_specs=[pl.BlockSpec(memory_space=pltpu.HBM)] * 7,
        out_specs=pl.BlockSpec(memory_space=pltpu.VMEM),
        scratch_shapes=[
            pltpu.VMEM((ROWS, HEADS, LAT), jnp.bfloat16),
            pltpu.VMEM((ROWS, HEADS * ROPE), jnp.bfloat16),
            pltpu.VMEM((ROWS, LAT), jnp.bfloat16),
            pltpu.VMEM((ROWS, ROPE), jnp.bfloat16),
            pltpu.VMEM((1, ROWS), jnp.int32),
            pltpu.VMEM((1, ROWS), jnp.float32),
            pltpu.VMEM((HEADS, LAT, VD), jnp.bfloat16),
            pltpu.VMEM((HEADS * ROWS, WIDE), jnp.bfloat16),
            pltpu.VMEM((KEYS, WIDE), jnp.bfloat16),
            pltpu.VMEM((ROWS, HEADS * VD), jnp.bfloat16),
            pltpu.VMEM((HEADS * ROWS, EARLY), jnp.float32),
            pltpu.VMEM((GROUP_ROWS, LAT), jnp.bfloat16),
            pltpu.SemaphoreType.DMA((6,)),
            pltpu.SemaphoreType.DMA((N_GROUPS,)),
            pltpu.SemaphoreType.DMA((NZ - 1,)),
            pltpu.SemaphoreType.DMA((NZ - 1,)),
            pltpu.SemaphoreType.DMA((NZ, 3)),
            pltpu.SemaphoreType.DMA((NZ, 3)),
            pltpu.SemaphoreType.DMA((NZ,)),
            pltpu.SemaphoreType.DMA((NZ,)),
            pltpu.SemaphoreType.DMA((HEADS // PIECE,)),
            pltpu.SemaphoreType.DMA((HEADS // PIECE,)),
        ],
        compiler_params=pltpu.CompilerParams(
            collective_id=0, has_side_effects=True, vmem_limit_bytes=56 * 2**20
        ),
        cost_estimate=pl.CostEstimate(flops=2_400_000_000, bytes_accessed=11_000_000, transcendentals=1_048_576),
        name="attend_and_hand_on",
    )(query_latent, query_rope, key_latent, key_rope, positions, router_weight, value_up)


def solution(mesh):
    placed = (
        P("pipe", "seq", None, None),
        P("pipe", "seq", None),
        P("pipe", "seq", None),
        P("pipe", "seq", None),
        P("pipe", "seq"),
        P("pipe", "seq"),
        P("pipe", None, None, None),
    )
    return jax.shard_map(
        on_device, mesh=mesh, in_specs=placed, out_specs=P("pipe", "seq", None), check_vma=False
    )
```

```python
import jax
import jax.numpy as jnp
from jax import lax
from jax.experimental import pallas as pl
from jax.experimental.pallas import tpu as pltpu
from jax.sharding import PartitionSpec as P

SCALE_LOG2E = 0.07216878364870322 * 1.4426950408889634
MASKED = -1.0e30
ROWS = 16
HEADS = 64
LAT = 512
ROPE = 64
VD = 128
NZ = 8
NY = 4
WIDE = LAT + 128
ZROW = NY * 2 * ROWS
KEYS = NZ * ZROW
GROUP = 16
GROUP_ROWS = GROUP * ROWS
N_GROUPS = HEADS // GROUP
PIECE = 16
MESH = pl.DeviceIdType.MESH
PLACE = {0: 0, 7: 1, 1: 2, 6: 3, 2: 4, 5: 5, 3: 6, 4: 7}
NEAR_FIRST = (7, 1, 6, 2, 5, 3, 4)
STEPS = (1, 2, 6, 3, 5, 4)
MID = 4
EARLY = 4 * ZROW


def body(
    ql_hbm, qr_hbm, kl_hbm, kr_hbm, pos_hbm, rw_hbm, vu_hbm, out,
    ql, qr, kl, kr, pos, rw, vu, q, kv, res, early, latents,
    local_sem, vu_sem, a_send, a_recv, y_send, y_recv, c_send, c_recv, x_send, x_recv,
):
    seq = lax.axis_index("seq")
    pipe = lax.axis_index("pipe")
    z = seq // (NY * 2)
    y = (seq // 2) % NY
    c = seq % 2

    def at(zz, yy, cc):
        return {"seq": (zz * NY + yy) * 2 + cc}

    def y_peer(dy):
        return at(z, (y + dy) % NY, c)

    sibling = at(z, y, 1 - c)
    after = {"pipe": (pipe + 1) % 4}
    before = {"pipe": (pipe + 3) % 4}

    barrier = pltpu.get_barrier_semaphore()
    for t in (7, 6, 5, 4, 3, 2, 1):

        @pl.when(z - t >= 0)
        def _():
            pl.semaphore_signal(barrier, inc=1, device_id=at(z - t, y, c), device_id_type=MESH)

    for dy in (1, 2, 3):
        pl.semaphore_signal(barrier, inc=1, device_id=y_peer(dy), device_id_type=MESH)
    pl.semaphore_signal(barrier, inc=1, device_id=sibling, device_id_type=MESH)
    pl.semaphore_signal(barrier, inc=1, device_id=before, device_id_type=MESH)

    loads = [
        pltpu.make_async_copy(kl_hbm.at[0], kl, local_sem.at[0]),
        pltpu.make_async_copy(kr_hbm.at[0], kr, local_sem.at[1]),
        pltpu.make_async_copy(pos_hbm, pos, local_sem.at[2]),
        pltpu.make_async_copy(rw_hbm, rw, local_sem.at[3]),
        pltpu.make_async_copy(ql_hbm.at[0], ql, local_sem.at[4]),
        pltpu.make_async_copy(qr_hbm.at[0], qr, local_sem.at[5]),
    ]
    for load in loads:
        load.start()

    def vu_load(g):
        return pltpu.make_async_copy(
            vu_hbm.at[0, pl.ds(g * GROUP, GROUP)], vu.at[pl.ds(g * GROUP, GROUP)], vu_sem.at[g]
        )

    diagonal = lax.broadcasted_iota(jnp.int32, (ROWS, ROWS), 0) == lax.broadcasted_iota(
        jnp.int32, (ROWS, ROWS), 1
    )
    for load in loads[:4]:
        load.wait()
    live_lane = jnp.where(pos[...] >= 0, 1.0, 0.0)
    live = jnp.sum(jnp.where(diagonal, live_lane, 0.0), axis=1, keepdims=True)
    gate = jnp.sum(jnp.where(diagonal, rw[...], 0.0), axis=1, keepdims=True) * live
    lane = lax.broadcasted_iota(jnp.int32, (ROWS, 128), 1)
    bias = jnp.where(live > 0.5, 0.0, MASKED)
    place = c * (NY * ROWS) + y * ROWS
    own_rows = pl.ds(pl.multiple_of(place, ROWS), ROWS)
    kv[own_rows, :LAT] = kl[...]
    kv[own_rows, LAT:] = jnp.where(
        lane < ROPE,
        jnp.concatenate([kr[...].astype(jnp.float32), jnp.zeros((ROWS, 128 - ROPE), jnp.float32)], axis=1),
        jnp.where(lane == ROPE, bias, 0.0),
    ).astype(jnp.bfloat16)

    tail_tile = jnp.where(lax.broadcasted_iota(jnp.int32, (ZROW, 128), 1) == ROPE, MASKED, 0.0).astype(jnp.bfloat16)
    for dz in NEAR_FIRST:

        @pl.when(z + dz < NZ)
        def _():
            rows = pl.ds(PLACE[dz] * ZROW, ZROW)
            kv[rows, :LAT] = jnp.zeros((ZROW, LAT), jnp.bfloat16)
            kv[rows, LAT:] = tail_tile

    for load in loads[4:]:
        load.wait()
    out_row = lax.broadcasted_iota(jnp.int32, (GROUP_ROWS, GROUP_ROWS), 0)
    in_row = lax.broadcasted_iota(jnp.int32, (GROUP_ROWS, GROUP_ROWS), 1)
    shuffle = ((out_row % ROWS) * GROUP + out_row // ROWS == in_row).astype(jnp.bfloat16)
    for g in range(N_GROUPS):
        block = ql[:, g * GROUP : (g + 1) * GROUP, :].reshape(GROUP_ROWS, LAT)
        q[g * GROUP_ROWS : (g + 1) * GROUP_ROWS, :LAT] = jnp.dot(
            shuffle, block, preferred_element_type=jnp.float32
        ).astype(jnp.bfloat16)
    for j in range(HEADS // 2):
        pair = qr[:, j * 128 : (j + 1) * 128].astype(jnp.float32)
        for odd in (0, 1):
            part = pltpu.roll(pair, ROPE, 1) if odd else pair
            part = jnp.where(lane < ROPE, part, jnp.where(lane == ROPE, 1.0, 0.0))
            h = 2 * j + odd
            q[h * ROWS : (h + 1) * ROWS, LAT:] = part.astype(jnp.bfloat16)

    key_slot = lax.broadcasted_iota(jnp.int32, (GROUP_ROWS, ZROW), 1)
    key_index = ((key_slot // ROWS) % NY) * (2 * ROWS) + (key_slot // (NY * ROWS)) * ROWS + key_slot % ROWS
    query_index = (y * 2 + c) * ROWS + lax.broadcasted_iota(jnp.int32, (GROUP_ROWS, ZROW), 0) % ROWS
    seen = key_index <= query_index

    pl.semaphore_wait(barrier, (NZ - 1 - z) + 5)

    def rows_of(dz):
        return pl.ds(pl.multiple_of(PLACE[dz] * ZROW + place, ROWS), ROWS)

    def half_of(dz, cc):
        return pl.ds(pl.multiple_of(PLACE[dz] * ZROW + cc * (NY * ROWS), ROWS), NY * ROWS)

    def a_copy(t):
        return pltpu.make_async_remote_copy(
            src_ref=kv.at[own_rows],
            dst_ref=kv.at[rows_of(NZ - t)],
            send_sem=a_send.at[t - 1],
            recv_sem=a_recv.at[NZ - t - 1],
            device_id=at(z + t, y, c),
            device_id_type=MESH,
        )

    def d_copy(t):
        return pltpu.make_async_remote_copy(
            src_ref=kv.at[half_of(0, c)],
            dst_ref=kv.at[half_of(NZ - t, c)],
            send_sem=a_send.at[t - 1],
            recv_sem=a_recv.at[NZ - t - 1],
            device_id=at(z + t, y, c),
            device_id_type=MESH,
        )

    def d_arrival(dz):
        return pltpu.make_async_remote_copy(
            src_ref=kv.at[half_of(0, c)],
            dst_ref=kv.at[half_of(dz, c)],
            send_sem=a_send.at[0],
            recv_sem=a_recv.at[dz - 1],
            device_id=sibling,
            device_id_type=MESH,
        )

    def a_arrival(dz):
        return pltpu.make_async_remote_copy(
            src_ref=kv.at[own_rows],
            dst_ref=kv.at[rows_of(dz)],
            send_sem=a_send.at[0],
            recv_sem=a_recv.at[dz - 1],
            device_id=sibling,
            device_id_type=MESH,
        )

    def y_copy(dz, dy):
        return pltpu.make_async_remote_copy(
            src_ref=kv.at[rows_of(dz)],
            dst_ref=kv.at[rows_of(dz)],
            send_sem=y_send.at[dz, dy - 1],
            recv_sem=y_recv.at[dz, dy - 1],
            device_id=y_peer(dy),
            device_id_type=MESH,
        )

    def c_copy(dz):
        return pltpu.make_async_remote_copy(
            src_ref=kv.at[half_of(dz, c)],
            dst_ref=kv.at[half_of(dz, c)],
            send_sem=c_send.at[dz],
            recv_sem=c_recv.at[dz],
            device_id=sibling,
            device_id_type=MESH,
        )

    def whole(dz, here):
        if dz == NZ - 1:
            return here >= MID
        if dz == 1:
            return here >= 0
        if dz == 2:
            return here < 0
        if dz == 6:
            return here < 0
        return here < 0

    def going(t, half):
        wanted = whole(NZ - t, z + t)
        return (z + t < NZ) & (wanted if half else jnp.logical_not(wanted))

    def coming(dz, half):
        wanted = whole(dz, z)
        return (z + dz >= NZ) & (wanted if half else jnp.logical_not(wanted))

    for t in STEPS:

        @pl.when(going(t, False))
        def _():
            a_copy(t).start()

    for dy in (2, 1, 3):
        y_copy(0, dy).start()
    for g in range(N_GROUPS):
        vu_load(g).start()

    def on_a(dz, now=True):
        @pl.when(coming(dz, False) & now)
        def _():
            a_arrival(dz).wait_recv()
            for dy in (2, 1, 3):
                y_copy(dz, dy).start()

    def on_y(dz, now=True):
        @pl.when(coming(dz, False) & now)
        def _():
            for dy in (2, 1, 3):
                y_copy(dz, dy).wait_recv()
            c_copy(dz).start()

    def on_d(dz):
        @pl.when(coming(dz, True))
        def _():
            d_arrival(dz).wait_recv()
            c_copy(dz).start()

    def on_c(dz):
        @pl.when(z + dz >= NZ)
        def _():
            c_copy(dz).wait_recv()

    on_a(7)
    for dy in (2, 1, 3):
        y_copy(0, dy).wait_recv()
    for t in (1, 7, 2, 6):

        @pl.when(going(t, True))
        def _():
            d_copy(t).start()

    c_copy(0).start()
    on_a(6)
    on_a(4, z == 5)
    for dz in (5, 2, 3):
        on_a(dz)
    on_a(4, z != 5)
    on_d(7)
    on_d(1)
    for dz in (7, 6, 2):
        on_y(dz)
    on_d(6)
    on_d(2)
    on_y(4, z == 5)
    for dz in (5, 3):
        on_y(dz)
    on_y(4, z != 5)
    c_copy(0).wait_recv()
    for dz in (7, 1, 6):
        on_c(dz)
    early[...] = lax.dot_general(
        q[...], kv[:EARLY], (((1,), (1,)), ((), ())), preferred_element_type=jnp.float32
    )
    for dz in (2, 5, 3, 4):
        on_c(dz)

    def x_copy(p):
        columns = pl.ds(pl.multiple_of(p * (PIECE * VD), 128), PIECE * VD)
        return pltpu.make_async_remote_copy(
            src_ref=res.at[:, columns],
            dst_ref=out.at[0, :, columns],
            send_sem=x_send.at[p],
            recv_sem=x_recv.at[p],
            device_id=after,
            device_id_type=MESH,
        )

    for g in range(N_GROUPS):
        vu_load(g).wait()

    @pl.loop(0, N_GROUPS)
    def _(g):
        rows = pl.ds(pl.multiple_of(g * GROUP_ROWS, GROUP_ROWS), GROUP_ROWS)

        def attend(scores, keys):
            top = jnp.max(scores, axis=1, keepdims=True)
            terms = jnp.exp2((scores - top) * SCALE_LOG2E)
            total = jnp.sum(terms, axis=1, keepdims=True)
            summed = jnp.dot(terms.astype(jnp.bfloat16), kv[:keys, :LAT], preferred_element_type=jnp.float32)
            latents[...] = (summed * (1.0 / jnp.maximum(total, 1.0))).astype(jnp.bfloat16)

        def first():
            return jnp.concatenate([jnp.where(seen, early[rows, :ZROW], MASKED), early[rows, ZROW:]], axis=1)

        @pl.when(z >= 3)
        def _():
            late = lax.dot_general(
                q[rows, :], kv[EARLY:], (((1,), (1,)), ((), ())), preferred_element_type=jnp.float32
            )
            attend(jnp.concatenate([first(), late], axis=1), KEYS)

        @pl.when(z < 3)
        def _():
            attend(first(), EARLY)

        latent = latents[...]
        for j in range(GROUP // 2):
            maps = vu[pl.ds(g * GROUP + 2 * j, 2)]
            both = jnp.concatenate([maps[0], maps[1]], axis=1)
            wide = jnp.dot(
                latent[2 * j * ROWS : (2 * j + 2) * ROWS], both, preferred_element_type=jnp.float32
            )
            piece = jnp.concatenate([wide[:ROWS, :VD], wide[ROWS:, VD:]], axis=1) * gate
            columns = pl.ds(pl.multiple_of((g * GROUP + 2 * j) * VD, 128), 2 * VD)
            res[:, columns] = piece.astype(jnp.bfloat16)
            if (2 * j + 2) % PIECE == 0:
                x_copy(g * (GROUP // PIECE) + (2 * j) // PIECE).start()

    for t in range(1, NZ):

        @pl.when(going(t, False))
        def _():
            a_copy(t).wait_send()

        @pl.when(going(t, True))
        def _():
            d_copy(t).wait_send()

    for dy in (2, 1, 3):
        y_copy(0, dy).wait_send()
    c_copy(0).wait_send()
    for dz in NEAR_FIRST:

        @pl.when(z + dz >= NZ)
        def _():
            c_copy(dz).wait_send()

        @pl.when(coming(dz, False))
        def _():
            for dy in (2, 1, 3):
                y_copy(dz, dy).wait_send()

    @pl.loop(0, HEADS // PIECE)
    def _(p):
        x_copy(p).wait()


def on_device(query_latent, query_rope, key_latent, key_rope, positions, router_weight, value_up):
    return pl.pallas_call(
        body,
        out_shape=pltpu.VMEM((1, ROWS, HEADS * VD), jnp.bfloat16),
        in_specs=[pl.BlockSpec(memory_space=pltpu.HBM)] * 7,
        out_specs=pl.BlockSpec(memory_space=pltpu.VMEM),
        scratch_shapes=[
            pltpu.VMEM((ROWS, HEADS, LAT), jnp.bfloat16),
            pltpu.VMEM((ROWS, HEADS * ROPE), jnp.bfloat16),
            pltpu.VMEM((ROWS, LAT), jnp.bfloat16),
            pltpu.VMEM((ROWS, ROPE), jnp.bfloat16),
            pltpu.VMEM((1, ROWS), jnp.int32),
            pltpu.VMEM((1, ROWS), jnp.float32),
            pltpu.VMEM((HEADS, LAT, VD), jnp.bfloat16),
            pltpu.VMEM((HEADS * ROWS, WIDE), jnp.bfloat16),
            pltpu.VMEM((KEYS, WIDE), jnp.bfloat16),
            pltpu.VMEM((ROWS, HEADS * VD), jnp.bfloat16),
            pltpu.VMEM((HEADS * ROWS, EARLY), jnp.float32),
            pltpu.VMEM((GROUP_ROWS, LAT), jnp.bfloat16),
            pltpu.SemaphoreType.DMA((6,)),
            pltpu.SemaphoreType.DMA((N_GROUPS,)),
            pltpu.SemaphoreType.DMA((NZ - 1,)),
            pltpu.SemaphoreType.DMA((NZ - 1,)),
            pltpu.SemaphoreType.DMA((NZ, 3)),
            pltpu.SemaphoreType.DMA((NZ, 3)),
            pltpu.SemaphoreType.DMA((NZ,)),
            pltpu.SemaphoreType.DMA((NZ,)),
            pltpu.SemaphoreType.DMA((HEADS // PIECE,)),
            pltpu.SemaphoreType.DMA((HEADS // PIECE,)),
        ],
        compiler_params=pltpu.CompilerParams(
            collective_id=0, has_side_effects=True, vmem_limit_bytes=56 * 2**20
        ),
        cost_estimate=pl.CostEstimate(flops=2_400_000_000, bytes_accessed=11_000_000, transcendentals=1_048_576),
        name="attend_and_hand_on",
    )(query_latent, query_rope, key_latent, key_rope, positions, router_weight, value_up)


def solution(mesh):
    placed = (
        P("pipe", "seq", None, None),
        P("pipe", "seq", None),
        P("pipe", "seq", None),
        P("pipe", "seq", None),
        P("pipe", "seq"),
        P("pipe", "seq"),
        P("pipe", None, None, None),
    )
    return jax.shard_map(
        on_device, mesh=mesh, in_specs=placed, out_specs=P("pipe", "seq", None), check_vma=False
    )
```

```python
import jax
import jax.numpy as jnp
from jax import lax
from jax.experimental import pallas as pl
from jax.experimental.pallas import tpu as pltpu
from jax.sharding import PartitionSpec as P

SCALE_LOG2E = 0.07216878364870322 * 1.4426950408889634
MASKED = -1.0e30
ROWS = 16
HEADS = 64
LAT = 512
ROPE = 64
VD = 128
NZ = 8
NY = 4
WIDE = LAT + 128
ZROW = NY * 2 * ROWS
KEYS = NZ * ZROW
GROUP = 16
GROUP_ROWS = GROUP * ROWS
N_GROUPS = HEADS // GROUP
PIECE = 16
MESH = pl.DeviceIdType.MESH
PLACE = {0: 0, 7: 1, 1: 2, 6: 3, 2: 4, 5: 5, 3: 6, 4: 7}
NEAR_FIRST = (7, 1, 6, 2, 5, 3, 4)
STEPS = (1, 2, 6, 3, 5, 4)
MID = 4
EARLY = 4 * ZROW


def body(
    ql_hbm, qr_hbm, kl_hbm, kr_hbm, pos_hbm, rw_hbm, vu_hbm, out,
    ql, qr, kl, kr, pos, rw, vu, q, kv, res, early, latents,
    local_sem, vu_sem, a_send, a_recv, y_send, y_recv, c_send, c_recv, x_send, x_recv,
):
    seq = lax.axis_index("seq")
    pipe = lax.axis_index("pipe")
    z = seq // (NY * 2)
    y = (seq // 2) % NY
    c = seq % 2

    def at(zz, yy, cc):
        return {"seq": (zz * NY + yy) * 2 + cc}

    def y_peer(dy):
        return at(z, (y + dy) % NY, c)

    sibling = at(z, y, 1 - c)
    after = {"pipe": (pipe + 1) % 4}
    before = {"pipe": (pipe + 3) % 4}

    barrier = pltpu.get_barrier_semaphore()
    for t in (7, 6, 5, 4, 3, 2, 1):

        @pl.when(z - t >= 0)
        def _():
            pl.semaphore_signal(barrier, inc=1, device_id=at(z - t, y, c), device_id_type=MESH)

    for dy in (1, 2, 3):
        pl.semaphore_signal(barrier, inc=1, device_id=y_peer(dy), device_id_type=MESH)
    pl.semaphore_signal(barrier, inc=1, device_id=sibling, device_id_type=MESH)
    pl.semaphore_signal(barrier, inc=1, device_id=before, device_id_type=MESH)

    loads = [
        pltpu.make_async_copy(kl_hbm.at[0], kl, local_sem.at[0]),
        pltpu.make_async_copy(kr_hbm.at[0], kr, local_sem.at[1]),
        pltpu.make_async_copy(pos_hbm, pos, local_sem.at[2]),
        pltpu.make_async_copy(rw_hbm, rw, local_sem.at[3]),
        pltpu.make_async_copy(ql_hbm.at[0], ql, local_sem.at[4]),
        pltpu.make_async_copy(qr_hbm.at[0], qr, local_sem.at[5]),
    ]
    for load in loads:
        load.start()

    def vu_load(g):
        return pltpu.make_async_copy(
            vu_hbm.at[0, pl.ds(g * GROUP, GROUP)], vu.at[pl.ds(g * GROUP, GROUP)], vu_sem.at[g]
        )

    diagonal = lax.broadcasted_iota(jnp.int32, (ROWS, ROWS), 0) == lax.broadcasted_iota(
        jnp.int32, (ROWS, ROWS), 1
    )
    for load in loads[:4]:
        load.wait()
    live_lane = jnp.where(pos[...] >= 0, 1.0, 0.0)
    live = jnp.sum(jnp.where(diagonal, live_lane, 0.0), axis=1, keepdims=True)
    gate = jnp.sum(jnp.where(diagonal, rw[...], 0.0), axis=1, keepdims=True) * live
    lane = lax.broadcasted_iota(jnp.int32, (ROWS, 128), 1)
    bias = jnp.where(live > 0.5, 0.0, MASKED)
    place = c * (NY * ROWS) + y * ROWS
    own_rows = pl.ds(pl.multiple_of(place, ROWS), ROWS)
    kv[own_rows, :LAT] = kl[...]
    kv[own_rows, LAT:] = jnp.where(
        lane < ROPE,
        jnp.concatenate([kr[...].astype(jnp.float32), jnp.zeros((ROWS, 128 - ROPE), jnp.float32)], axis=1),
        jnp.where(lane == ROPE, bias, 0.0),
    ).astype(jnp.bfloat16)

    tail_tile = jnp.where(lax.broadcasted_iota(jnp.int32, (ZROW, 128), 1) == ROPE, MASKED, 0.0).astype(jnp.bfloat16)
    for dz in NEAR_FIRST:

        @pl.when(z + dz < NZ)
        def _():
            rows = pl.ds(PLACE[dz] * ZROW, ZROW)
            kv[rows, :LAT] = jnp.zeros((ZROW, LAT), jnp.bfloat16)
            kv[rows, LAT:] = tail_tile

    for load in loads[4:]:
        load.wait()
    out_row = lax.broadcasted_iota(jnp.int32, (GROUP_ROWS, GROUP_ROWS), 0)
    in_row = lax.broadcasted_iota(jnp.int32, (GROUP_ROWS, GROUP_ROWS), 1)
    shuffle = ((out_row % ROWS) * GROUP + out_row // ROWS == in_row).astype(jnp.bfloat16)
    for g in range(N_GROUPS):
        block = ql[:, g * GROUP : (g + 1) * GROUP, :].reshape(GROUP_ROWS, LAT)
        q[g * GROUP_ROWS : (g + 1) * GROUP_ROWS, :LAT] = jnp.dot(
            shuffle, block, preferred_element_type=jnp.float32
        ).astype(jnp.bfloat16)
    for j in range(HEADS // 2):
        pair = qr[:, j * 128 : (j + 1) * 128].astype(jnp.float32)
        for odd in (0, 1):
            part = pltpu.roll(pair, ROPE, 1) if odd else pair
            part = jnp.where(lane < ROPE, part, jnp.where(lane == ROPE, 1.0, 0.0))
            h = 2 * j + odd
            q[h * ROWS : (h + 1) * ROWS, LAT:] = part.astype(jnp.bfloat16)

    key_slot = lax.broadcasted_iota(jnp.int32, (GROUP_ROWS, ZROW), 1)
    key_index = ((key_slot // ROWS) % NY) * (2 * ROWS) + (key_slot // (NY * ROWS)) * ROWS + key_slot % ROWS
    query_index = (y * 2 + c) * ROWS + lax.broadcasted_iota(jnp.int32, (GROUP_ROWS, ZROW), 0) % ROWS
    seen = key_index <= query_index

    pl.semaphore_wait(barrier, (NZ - 1 - z) + 5)

    def rows_of(dz):
        return pl.ds(pl.multiple_of(PLACE[dz] * ZROW + place, ROWS), ROWS)

    def half_of(dz, cc):
        return pl.ds(pl.multiple_of(PLACE[dz] * ZROW + cc * (NY * ROWS), ROWS), NY * ROWS)

    def a_copy(t):
        return pltpu.make_async_remote_copy(
            src_ref=kv.at[own_rows],
            dst_ref=kv.at[rows_of(NZ - t)],
            send_sem=a_send.at[t - 1],
            recv_sem=a_recv.at[NZ - t - 1],
            device_id=at(z + t, y, c),
            device_id_type=MESH,
        )

    def d_copy(t):
        return pltpu.make_async_remote_copy(
            src_ref=kv.at[half_of(0, c)],
            dst_ref=kv.at[half_of(NZ - t, c)],
            send_sem=a_send.at[t - 1],
            recv_sem=a_recv.at[NZ - t - 1],
            device_id=at(z + t, y, c),
            device_id_type=MESH,
        )

    def d_arrival(dz):
        return pltpu.make_async_remote_copy(
            src_ref=kv.at[half_of(0, c)],
            dst_ref=kv.at[half_of(dz, c)],
            send_sem=a_send.at[0],
            recv_sem=a_recv.at[dz - 1],
            device_id=sibling,
            device_id_type=MESH,
        )

    def a_arrival(dz):
        return pltpu.make_async_remote_copy(
            src_ref=kv.at[own_rows],
            dst_ref=kv.at[rows_of(dz)],
            send_sem=a_send.at[0],
            recv_sem=a_recv.at[dz - 1],
            device_id=sibling,
            device_id_type=MESH,
        )

    def y_copy(dz, dy):
        return pltpu.make_async_remote_copy(
            src_ref=kv.at[rows_of(dz)],
            dst_ref=kv.at[rows_of(dz)],
            send_sem=y_send.at[dz, dy - 1],
            recv_sem=y_recv.at[dz, dy - 1],
            device_id=y_peer(dy),
            device_id_type=MESH,
        )

    def c_copy(dz):
        return pltpu.make_async_remote_copy(
            src_ref=kv.at[half_of(dz, c)],
            dst_ref=kv.at[half_of(dz, c)],
            send_sem=c_send.at[dz],
            recv_sem=c_recv.at[dz],
            device_id=sibling,
            device_id_type=MESH,
        )

    def whole(dz, here):
        if dz == NZ - 1:
            return here >= MID
        if dz == 1:
            return here >= 0
        if dz == 2:
            return here < 0
        if dz == 6:
            return here < 0
        return here < 0

    def going(t, half):
        wanted = whole(NZ - t, z + t)
        return (z + t < NZ) & (wanted if half else jnp.logical_not(wanted))

    def coming(dz, half):
        wanted = whole(dz, z)
        return (z + dz >= NZ) & (wanted if half else jnp.logical_not(wanted))

    for t, now in ((1, True), (2, True), (6, True), (4, z == 2), (3, True), (5, True), (4, z != 2)):

        @pl.when(going(t, False) & now)
        def _():
            a_copy(t).start()

    for dy in (2, 1, 3):
        y_copy(0, dy).start()
    for g in range(N_GROUPS):
        vu_load(g).start()

    def on_a(dz, now=True):
        @pl.when(coming(dz, False) & now)
        def _():
            a_arrival(dz).wait_recv()
            for dy in (2, 1, 3):
                y_copy(dz, dy).start()

    def on_y(dz, now=True):
        @pl.when(coming(dz, False) & now)
        def _():
            for dy in (2, 1, 3):
                y_copy(dz, dy).wait_recv()
            c_copy(dz).start()

    def on_d(dz):
        @pl.when(coming(dz, True))
        def _():
            d_arrival(dz).wait_recv()
            c_copy(dz).start()

    def on_c(dz):
        @pl.when(z + dz >= NZ)
        def _():
            c_copy(dz).wait_recv()

    on_a(7)
    for dy in (2, 1, 3):
        y_copy(0, dy).wait_recv()
    for t in (1, 7, 2, 6):

        @pl.when(going(t, True))
        def _():
            d_copy(t).start()

    c_copy(0).start()
    on_a(6)
    on_a(4, z == 5)
    for dz in (5, 2, 3):
        on_a(dz)
    on_a(4, z != 5)
    on_d(7)
    on_d(1)
    for dz in (7, 6, 2):
        on_y(dz)
    on_d(6)
    on_d(2)
    on_y(4, z == 5)
    for dz in (5, 3):
        on_y(dz)
    on_y(4, z != 5)
    c_copy(0).wait_recv()
    for dz in (7, 1, 6):
        on_c(dz)
    early[...] = lax.dot_general(
        q[...], kv[:EARLY], (((1,), (1,)), ((), ())), preferred_element_type=jnp.float32
    )
    for dz in (2, 5, 3, 4):
        on_c(dz)

    def x_copy(p):
        columns = pl.ds(pl.multiple_of(p * (PIECE * VD), 128), PIECE * VD)
        return pltpu.make_async_remote_copy(
            src_ref=res.at[:, columns],
            dst_ref=out.at[0, :, columns],
            send_sem=x_send.at[p],
            recv_sem=x_recv.at[p],
            device_id=after,
            device_id_type=MESH,
        )

    for g in range(N_GROUPS):
        vu_load(g).wait()

    @pl.loop(0, N_GROUPS)
    def _(g):
        rows = pl.ds(pl.multiple_of(g * GROUP_ROWS, GROUP_ROWS), GROUP_ROWS)

        def attend(scores, keys):
            top = jnp.max(scores, axis=1, keepdims=True)
            terms = jnp.exp2((scores - top) * SCALE_LOG2E)
            total = jnp.sum(terms, axis=1, keepdims=True)
            summed = jnp.dot(terms.astype(jnp.bfloat16), kv[:keys, :LAT], preferred_element_type=jnp.float32)
            latents[...] = (summed * (1.0 / jnp.maximum(total, 1.0))).astype(jnp.bfloat16)

        def first():
            return jnp.concatenate([jnp.where(seen, early[rows, :ZROW], MASKED), early[rows, ZROW:]], axis=1)

        @pl.when(z >= 3)
        def _():
            late = lax.dot_general(
                q[rows, :], kv[EARLY:], (((1,), (1,)), ((), ())), preferred_element_type=jnp.float32
            )
            attend(jnp.concatenate([first(), late], axis=1), KEYS)

        @pl.when(z < 3)
        def _():
            attend(first(), EARLY)

        latent = latents[...]
        for j in range(GROUP // 2):
            maps = vu[pl.ds(g * GROUP + 2 * j, 2)]
            both = jnp.concatenate([maps[0], maps[1]], axis=1)
            wide = jnp.dot(
                latent[2 * j * ROWS : (2 * j + 2) * ROWS], both, preferred_element_type=jnp.float32
            )
            piece = jnp.concatenate([wide[:ROWS, :VD], wide[ROWS:, VD:]], axis=1) * gate
            columns = pl.ds(pl.multiple_of((g * GROUP + 2 * j) * VD, 128), 2 * VD)
            res[:, columns] = piece.astype(jnp.bfloat16)
            if (2 * j + 2) % PIECE == 0:
                x_copy(g * (GROUP // PIECE) + (2 * j) // PIECE).start()

    for t in range(1, NZ):

        @pl.when(going(t, False))
        def _():
            a_copy(t).wait_send()

        @pl.when(going(t, True))
        def _():
            d_copy(t).wait_send()

    for dy in (2, 1, 3):
        y_copy(0, dy).wait_send()
    c_copy(0).wait_send()
    for dz in NEAR_FIRST:

        @pl.when(z + dz >= NZ)
        def _():
            c_copy(dz).wait_send()

        @pl.when(coming(dz, False))
        def _():
            for dy in (2, 1, 3):
                y_copy(dz, dy).wait_send()

    @pl.loop(0, HEADS // PIECE)
    def _(p):
        x_copy(p).wait()


def on_device(query_latent, query_rope, key_latent, key_rope, positions, router_weight, value_up):
    return pl.pallas_call(
        body,
        out_shape=pltpu.VMEM((1, ROWS, HEADS * VD), jnp.bfloat16),
        in_specs=[pl.BlockSpec(memory_space=pltpu.HBM)] * 7,
        out_specs=pl.BlockSpec(memory_space=pltpu.VMEM),
        scratch_shapes=[
            pltpu.VMEM((ROWS, HEADS, LAT), jnp.bfloat16),
            pltpu.VMEM((ROWS, HEADS * ROPE), jnp.bfloat16),
            pltpu.VMEM((ROWS, LAT), jnp.bfloat16),
            pltpu.VMEM((ROWS, ROPE), jnp.bfloat16),
            pltpu.VMEM((1, ROWS), jnp.int32),
            pltpu.VMEM((1, ROWS), jnp.float32),
            pltpu.VMEM((HEADS, LAT, VD), jnp.bfloat16),
            pltpu.VMEM((HEADS * ROWS, WIDE), jnp.bfloat16),
            pltpu.VMEM((KEYS, WIDE), jnp.bfloat16),
            pltpu.VMEM((ROWS, HEADS * VD), jnp.bfloat16),
            pltpu.VMEM((HEADS * ROWS, EARLY), jnp.float32),
            pltpu.VMEM((GROUP_ROWS, LAT), jnp.bfloat16),
            pltpu.SemaphoreType.DMA((6,)),
            pltpu.SemaphoreType.DMA((N_GROUPS,)),
            pltpu.SemaphoreType.DMA((NZ - 1,)),
            pltpu.SemaphoreType.DMA((NZ - 1,)),
            pltpu.SemaphoreType.DMA((NZ, 3)),
            pltpu.SemaphoreType.DMA((NZ, 3)),
            pltpu.SemaphoreType.DMA((NZ,)),
            pltpu.SemaphoreType.DMA((NZ,)),
            pltpu.SemaphoreType.DMA((HEADS // PIECE,)),
            pltpu.SemaphoreType.DMA((HEADS // PIECE,)),
        ],
        compiler_params=pltpu.CompilerParams(
            collective_id=0, has_side_effects=True, vmem_limit_bytes=56 * 2**20
        ),
        cost_estimate=pl.CostEstimate(flops=2_400_000_000, bytes_accessed=11_000_000, transcendentals=1_048_576),
        name="attend_and_hand_on",
    )(query_latent, query_rope, key_latent, key_rope, positions, router_weight, value_up)


def solution(mesh):
    placed = (
        P("pipe", "seq", None, None),
        P("pipe", "seq", None),
        P("pipe", "seq", None),
        P("pipe", "seq", None),
        P("pipe", "seq"),
        P("pipe", "seq"),
        P("pipe", None, None, None),
    )
    return jax.shard_map(
        on_device, mesh=mesh, in_specs=placed, out_specs=P("pipe", "seq", None), check_vma=False
    )
```

```python
import jax
import jax.numpy as jnp
from jax import lax
from jax.experimental import pallas as pl
from jax.experimental.pallas import tpu as pltpu
from jax.sharding import PartitionSpec as P

SCALE_LOG2E = 0.07216878364870322 * 1.4426950408889634
MASKED = -1.0e30
ROWS = 16
HEADS = 64
LAT = 512
ROPE = 64
VD = 128
NZ = 8
NY = 4
WIDE = LAT + 128
ZROW = NY * 2 * ROWS
KEYS = NZ * ZROW
GROUP = 16
GROUP_ROWS = GROUP * ROWS
N_GROUPS = HEADS // GROUP
PIECE = 16
MESH = pl.DeviceIdType.MESH
PLACE = {0: 0, 7: 1, 1: 2, 6: 3, 2: 4, 5: 5, 3: 6, 4: 7}
NEAR_FIRST = (7, 1, 6, 2, 5, 3, 4)
STEPS = (1, 2, 6, 3, 5, 4)
MID = 4
EARLY = 4 * ZROW


def body(
    ql_hbm, qr_hbm, kl_hbm, kr_hbm, pos_hbm, rw_hbm, vu_hbm, out,
    ql, qr, kl, kr, pos, rw, vu, q, kv, res, early, latents,
    local_sem, vu_sem, a_send, a_recv, y_send, y_recv, c_send, c_recv, x_send, x_recv,
):
    seq = lax.axis_index("seq")
    pipe = lax.axis_index("pipe")
    z = seq // (NY * 2)
    y = (seq // 2) % NY
    c = seq % 2

    def at(zz, yy, cc):
        return {"seq": (zz * NY + yy) * 2 + cc}

    def y_peer(dy):
        return at(z, (y + dy) % NY, c)

    sibling = at(z, y, 1 - c)
    after = {"pipe": (pipe + 1) % 4}
    before = {"pipe": (pipe + 3) % 4}

    barrier = pltpu.get_barrier_semaphore()
    for t in (7, 6, 5, 4, 3, 2, 1):

        @pl.when(z - t >= 0)
        def _():
            pl.semaphore_signal(barrier, inc=1, device_id=at(z - t, y, c), device_id_type=MESH)

    for dy in (1, 2, 3):
        pl.semaphore_signal(barrier, inc=1, device_id=y_peer(dy), device_id_type=MESH)
    pl.semaphore_signal(barrier, inc=1, device_id=sibling, device_id_type=MESH)
    pl.semaphore_signal(barrier, inc=1, device_id=before, device_id_type=MESH)

    loads = [
        pltpu.make_async_copy(kl_hbm.at[0], kl, local_sem.at[0]),
        pltpu.make_async_copy(kr_hbm.at[0], kr, local_sem.at[1]),
        pltpu.make_async_copy(pos_hbm, pos, local_sem.at[2]),
        pltpu.make_async_copy(rw_hbm, rw, local_sem.at[3]),
        pltpu.make_async_copy(ql_hbm.at[0], ql, local_sem.at[4]),
        pltpu.make_async_copy(qr_hbm.at[0], qr, local_sem.at[5]),
    ]
    for load in loads:
        load.start()

    def vu_load(g):
        return pltpu.make_async_copy(
            vu_hbm.at[0, pl.ds(g * GROUP, GROUP)], vu.at[pl.ds(g * GROUP, GROUP)], vu_sem.at[g]
        )

    diagonal = lax.broadcasted_iota(jnp.int32, (ROWS, ROWS), 0) == lax.broadcasted_iota(
        jnp.int32, (ROWS, ROWS), 1
    )
    for load in loads[:4]:
        load.wait()
    live_lane = jnp.where(pos[...] >= 0, 1.0, 0.0)
    live = jnp.sum(jnp.where(diagonal, live_lane, 0.0), axis=1, keepdims=True)
    gate = jnp.sum(jnp.where(diagonal, rw[...], 0.0), axis=1, keepdims=True) * live
    lane = lax.broadcasted_iota(jnp.int32, (ROWS, 128), 1)
    bias = jnp.where(live > 0.5, 0.0, MASKED)
    place = c * (NY * ROWS) + y * ROWS
    own_rows = pl.ds(pl.multiple_of(place, ROWS), ROWS)
    kv[own_rows, :LAT] = kl[...]
    kv[own_rows, LAT:] = jnp.where(
        lane < ROPE,
        jnp.concatenate([kr[...].astype(jnp.float32), jnp.zeros((ROWS, 128 - ROPE), jnp.float32)], axis=1),
        jnp.where(lane == ROPE, bias, 0.0),
    ).astype(jnp.bfloat16)

    tail_tile = jnp.where(lax.broadcasted_iota(jnp.int32, (ZROW, 128), 1) == ROPE, MASKED, 0.0).astype(jnp.bfloat16)
    for dz in NEAR_FIRST:

        @pl.when(z + dz < NZ)
        def _():
            rows = pl.ds(PLACE[dz] * ZROW, ZROW)
            kv[rows, :LAT] = jnp.zeros((ZROW, LAT), jnp.bfloat16)
            kv[rows, LAT:] = tail_tile

    for load in loads[4:]:
        load.wait()
    out_row = lax.broadcasted_iota(jnp.int32, (GROUP_ROWS, GROUP_ROWS), 0)
    in_row = lax.broadcasted_iota(jnp.int32, (GROUP_ROWS, GROUP_ROWS), 1)
    shuffle = ((out_row % ROWS) * GROUP + out_row // ROWS == in_row).astype(jnp.bfloat16)
    for g in range(N_GROUPS):
        block = ql[:, g * GROUP : (g + 1) * GROUP, :].reshape(GROUP_ROWS, LAT)
        q[g * GROUP_ROWS : (g + 1) * GROUP_ROWS, :LAT] = jnp.dot(
            shuffle, block, preferred_element_type=jnp.float32
        ).astype(jnp.bfloat16)
    for j in range(HEADS // 2):
        pair = qr[:, j * 128 : (j + 1) * 128].astype(jnp.float32)
        for odd in (0, 1):
            part = pltpu.roll(pair, ROPE, 1) if odd else pair
            part = jnp.where(lane < ROPE, part, jnp.where(lane == ROPE, 1.0, 0.0))
            h = 2 * j + odd
            q[h * ROWS : (h + 1) * ROWS, LAT:] = part.astype(jnp.bfloat16)

    key_slot = lax.broadcasted_iota(jnp.int32, (GROUP_ROWS, ZROW), 1)
    key_index = ((key_slot // ROWS) % NY) * (2 * ROWS) + (key_slot // (NY * ROWS)) * ROWS + key_slot % ROWS
    query_index = (y * 2 + c) * ROWS + lax.broadcasted_iota(jnp.int32, (GROUP_ROWS, ZROW), 0) % ROWS
    seen = key_index <= query_index

    pl.semaphore_wait(barrier, (NZ - 1 - z) + 5)

    def rows_of(dz):
        return pl.ds(pl.multiple_of(PLACE[dz] * ZROW + place, ROWS), ROWS)

    def half_of(dz, cc):
        return pl.ds(pl.multiple_of(PLACE[dz] * ZROW + cc * (NY * ROWS), ROWS), NY * ROWS)

    def a_copy(t):
        return pltpu.make_async_remote_copy(
            src_ref=kv.at[own_rows],
            dst_ref=kv.at[rows_of(NZ - t)],
            send_sem=a_send.at[t - 1],
            recv_sem=a_recv.at[NZ - t - 1],
            device_id=at(z + t, y, c),
            device_id_type=MESH,
        )

    def d_copy(t):
        return pltpu.make_async_remote_copy(
            src_ref=kv.at[half_of(0, c)],
            dst_ref=kv.at[half_of(NZ - t, c)],
            send_sem=a_send.at[t - 1],
            recv_sem=a_recv.at[NZ - t - 1],
            device_id=at(z + t, y, c),
            device_id_type=MESH,
        )

    def d_arrival(dz):
        return pltpu.make_async_remote_copy(
            src_ref=kv.at[half_of(0, c)],
            dst_ref=kv.at[half_of(dz, c)],
            send_sem=a_send.at[0],
            recv_sem=a_recv.at[dz - 1],
            device_id=sibling,
            device_id_type=MESH,
        )

    def a_arrival(dz):
        return pltpu.make_async_remote_copy(
            src_ref=kv.at[own_rows],
            dst_ref=kv.at[rows_of(dz)],
            send_sem=a_send.at[0],
            recv_sem=a_recv.at[dz - 1],
            device_id=sibling,
            device_id_type=MESH,
        )

    def y_copy(dz, dy):
        return pltpu.make_async_remote_copy(
            src_ref=kv.at[rows_of(dz)],
            dst_ref=kv.at[rows_of(dz)],
            send_sem=y_send.at[dz, dy - 1],
            recv_sem=y_recv.at[dz, dy - 1],
            device_id=y_peer(dy),
            device_id_type=MESH,
        )

    def c_copy(dz):
        return pltpu.make_async_remote_copy(
            src_ref=kv.at[half_of(dz, c)],
            dst_ref=kv.at[half_of(dz, c)],
            send_sem=c_send.at[dz],
            recv_sem=c_recv.at[dz],
            device_id=sibling,
            device_id_type=MESH,
        )

    def whole(dz, here):
        if dz == NZ - 1:
            return here >= MID
        if dz == 1:
            return here >= 0
        if dz == 2:
            return here < 0
        if dz == 6:
            return here < 0
        return here < 0

    def going(t, half):
        wanted = whole(NZ - t, z + t)
        return (z + t < NZ) & (wanted if half else jnp.logical_not(wanted))

    def coming(dz, half):
        wanted = whole(dz, z)
        return (z + dz >= NZ) & (wanted if half else jnp.logical_not(wanted))

    for t, now in ((1, True), (2, True), (6, True), (4, z == 2), (3, True), (5, True), (4, z != 2)):

        @pl.when(going(t, False) & now)
        def _():
            a_copy(t).start()

    for dy in (2, 1, 3):
        y_copy(0, dy).start()
    for g in range(N_GROUPS):
        vu_load(g).start()

    def on_a(dz, now=True):
        @pl.when(coming(dz, False) & now)
        def _():
            a_arrival(dz).wait_recv()
            for dy in (2, 1, 3):
                y_copy(dz, dy).start()

    def on_y(dz, now=True):
        @pl.when(coming(dz, False) & now)
        def _():
            for dy in (2, 1, 3):
                y_copy(dz, dy).wait_recv()
            c_copy(dz).start()

    def on_d(dz):
        @pl.when(coming(dz, True))
        def _():
            d_arrival(dz).wait_recv()
            c_copy(dz).start()

    def on_c(dz):
        @pl.when(z + dz >= NZ)
        def _():
            c_copy(dz).wait_recv()

    on_a(7)
    for dy in (2, 1, 3):
        y_copy(0, dy).wait_recv()
    for t in (1, 7, 2, 6):

        @pl.when(going(t, True))
        def _():
            d_copy(t).start()

    c_copy(0).start()
    on_a(6)
    on_a(4, z == 5)
    on_a(3, z == 6)
    for dz in (5, 2):
        on_a(dz)
    on_a(3, z != 6)
    on_a(4, z != 5)
    on_d(7)
    on_d(1)
    for dz in (7, 6, 2):
        on_y(dz)
    on_d(6)
    on_d(2)
    on_y(4, z == 5)
    on_y(3, z == 6)
    on_y(5)
    on_y(3, z != 6)
    on_y(4, z != 5)
    c_copy(0).wait_recv()
    for dz in (7, 1, 6):
        on_c(dz)
    early[...] = lax.dot_general(
        q[...], kv[:EARLY], (((1,), (1,)), ((), ())), preferred_element_type=jnp.float32
    )
    for dz in (2, 5, 3, 4):
        on_c(dz)

    def x_copy(p):
        columns = pl.ds(pl.multiple_of(p * (PIECE * VD), 128), PIECE * VD)
        return pltpu.make_async_remote_copy(
            src_ref=res.at[:, columns],
            dst_ref=out.at[0, :, columns],
            send_sem=x_send.at[p],
            recv_sem=x_recv.at[p],
            device_id=after,
            device_id_type=MESH,
        )

    for g in range(N_GROUPS):
        vu_load(g).wait()

    @pl.loop(0, N_GROUPS)
    def _(g):
        rows = pl.ds(pl.multiple_of(g * GROUP_ROWS, GROUP_ROWS), GROUP_ROWS)

        def attend(scores, keys):
            top = jnp.max(scores, axis=1, keepdims=True)
            terms = jnp.exp2((scores - top) * SCALE_LOG2E)
            total = jnp.sum(terms, axis=1, keepdims=True)
            summed = jnp.dot(terms.astype(jnp.bfloat16), kv[:keys, :LAT], preferred_element_type=jnp.float32)
            latents[...] = (summed * (1.0 / jnp.maximum(total, 1.0))).astype(jnp.bfloat16)

        def first():
            return jnp.concatenate([jnp.where(seen, early[rows, :ZROW], MASKED), early[rows, ZROW:]], axis=1)

        @pl.when(z >= 3)
        def _():
            late = lax.dot_general(
                q[rows, :], kv[EARLY:], (((1,), (1,)), ((), ())), preferred_element_type=jnp.float32
            )
            attend(jnp.concatenate([first(), late], axis=1), KEYS)

        @pl.when(z < 3)
        def _():
            attend(first(), EARLY)

        latent = latents[...]
        for j in range(GROUP // 2):
            maps = vu[pl.ds(g * GROUP + 2 * j, 2)]
            both = jnp.concatenate([maps[0], maps[1]], axis=1)
            wide = jnp.dot(
                latent[2 * j * ROWS : (2 * j + 2) * ROWS], both, preferred_element_type=jnp.float32
            )
            piece = jnp.concatenate([wide[:ROWS, :VD], wide[ROWS:, VD:]], axis=1) * gate
            columns = pl.ds(pl.multiple_of((g * GROUP + 2 * j) * VD, 128), 2 * VD)
            res[:, columns] = piece.astype(jnp.bfloat16)
            if (2 * j + 2) % PIECE == 0:
                x_copy(g * (GROUP // PIECE) + (2 * j) // PIECE).start()

    for t in range(1, NZ):

        @pl.when(going(t, False))
        def _():
            a_copy(t).wait_send()

        @pl.when(going(t, True))
        def _():
            d_copy(t).wait_send()

    for dy in (2, 1, 3):
        y_copy(0, dy).wait_send()
    c_copy(0).wait_send()
    for dz in NEAR_FIRST:

        @pl.when(z + dz >= NZ)
        def _():
            c_copy(dz).wait_send()

        @pl.when(coming(dz, False))
        def _():
            for dy in (2, 1, 3):
                y_copy(dz, dy).wait_send()

    @pl.loop(0, HEADS // PIECE)
    def _(p):
        x_copy(p).wait()


def on_device(query_latent, query_rope, key_latent, key_rope, positions, router_weight, value_up):
    return pl.pallas_call(
        body,
        out_shape=pltpu.VMEM((1, ROWS, HEADS * VD), jnp.bfloat16),
        in_specs=[pl.BlockSpec(memory_space=pltpu.HBM)] * 7,
        out_specs=pl.BlockSpec(memory_space=pltpu.VMEM),
        scratch_shapes=[
            pltpu.VMEM((ROWS, HEADS, LAT), jnp.bfloat16),
            pltpu.VMEM((ROWS, HEADS * ROPE), jnp.bfloat16),
            pltpu.VMEM((ROWS, LAT), jnp.bfloat16),
            pltpu.VMEM((ROWS, ROPE), jnp.bfloat16),
            pltpu.VMEM((1, ROWS), jnp.int32),
            pltpu.VMEM((1, ROWS), jnp.float32),
            pltpu.VMEM((HEADS, LAT, VD), jnp.bfloat16),
            pltpu.VMEM((HEADS * ROWS, WIDE), jnp.bfloat16),
            pltpu.VMEM((KEYS, WIDE), jnp.bfloat16),
            pltpu.VMEM((ROWS, HEADS * VD), jnp.bfloat16),
            pltpu.VMEM((HEADS * ROWS, EARLY), jnp.float32),
            pltpu.VMEM((GROUP_ROWS, LAT), jnp.bfloat16),
            pltpu.SemaphoreType.DMA((6,)),
            pltpu.SemaphoreType.DMA((N_GROUPS,)),
            pltpu.SemaphoreType.DMA((NZ - 1,)),
            pltpu.SemaphoreType.DMA((NZ - 1,)),
            pltpu.SemaphoreType.DMA((NZ, 3)),
            pltpu.SemaphoreType.DMA((NZ, 3)),
            pltpu.SemaphoreType.DMA((NZ,)),
            pltpu.SemaphoreType.DMA((NZ,)),
            pltpu.SemaphoreType.DMA((HEADS // PIECE,)),
            pltpu.SemaphoreType.DMA((HEADS // PIECE,)),
        ],
        compiler_params=pltpu.CompilerParams(
            collective_id=0, has_side_effects=True, vmem_limit_bytes=56 * 2**20
        ),
        cost_estimate=pl.CostEstimate(flops=2_400_000_000, bytes_accessed=11_000_000, transcendentals=1_048_576),
        name="attend_and_hand_on",
    )(query_latent, query_rope, key_latent, key_rope, positions, router_weight, value_up)


def solution(mesh):
    placed = (
        P("pipe", "seq", None, None),
        P("pipe", "seq", None),
        P("pipe", "seq", None),
        P("pipe", "seq", None),
        P("pipe", "seq"),
        P("pipe", "seq"),
        P("pipe", None, None, None),
    )
    return jax.shard_map(
        on_device, mesh=mesh, in_specs=placed, out_specs=P("pipe", "seq", None), check_vma=False
    )
```
